32 devices in a mesh: section: 2 (over core), dp: 16 (over z, y, x).
Axes of the slice: x: 2, y: 2, z: 4, core: 2. Of those that a mesh axis runs over, the one named last changes fastest.
Arguments:
- tokens: bfloat16 [65536, 512], P('dp'), may hold values from -6 to 6
- lengths: int32 [32, 3], P('dp'), may hold values from 1 to 32, 64 in all within a row
- w_qkv: bfloat16 [512, 1536], replicated, may hold values from -0.25 to 0.25
- w_out: bfloat16 [512, 512], replicated, may hold values from -0.75 to 0.75
- w_sort: bfloat16 [512, 256], replicated, may hold values from -2.5 to 2.5
- gain_attn: float32 [512], replicated, may hold values from 0.5 to 1.5
- bias_attn: float32 [512], replicated, may hold values from -1.5 to 1.5
- gain_ffn: float32 [512], replicated, may hold values from 0.5 to 1.5
- bias_ffn: float32 [512], replicated, may hold values from -1.5 to 1.5
- w_up: bfloat16 [512, 2048], replicated, may hold values from -0.25 to 0.25
- bias_up: float32 [2048], replicated, may hold values from -1.5 to 1.5
- w_down: bfloat16 [2048, 512], replicated, may hold values from -0.125 to 0.125
- bias_down: float32 [512], replicated, may hold values from -1.5 to 1.5
- cotangent: bfloat16 [65536, 512], P('dp'), may hold values from -6 to 6
Outputs:
- ends: float32 [2, 65536, 512], P('section', 'dp')
- grad_qkv: float32 [512, 1536], replicated
- grad_out: float32 [512, 512], replicated
- grad_sort: float32 [512, 256], replicated
- grad_gain_attn: float32 [512], replicated
- grad_bias_attn: float32 [512], replicated
- grad_gain_ffn: float32 [512], replicated
- grad_bias_ffn: float32 [512], replicated
- grad_up: float32 [512, 2048], replicated
- grad_bias_up: float32 [2048], replicated
- grad_down: float32 [2048, 512], replicated
- grad_bias_down: float32 [512], replicated
The draws below stay inside these ranges and needn't reach their ends.
Inputs may be any that keep to these rules, and one draw needn't show every extreme that they name: lengths in blocks of 32 tokens; each row sums to 64, and its longest sequence has exactly 32 blocks.
All inputs are finite; a program needn't handle non-finite values.
Results may differ from the reference program's by a relative error of at most 0.017.
Values may be sent and summed in bfloat16 or wider, within the bound.
A program may use at most 256 MiB of HBM per device.

```python
import math
import jax
import jax.numpy as jnp
import numpy as np
from jax import lax

D = 512
HEADS = 8
HDIM = 64
FF = 2048
BLK = 32
SINK = 8
SEQS = 3
MB = 2048
NBLK = 64
SPAN = 32
ROWS = 32
TOKENS = 65536


def shard_levels(stream_key, shape, pieces, least, high):
    gain = 1.0
    for position, parts in pieces:
        steps = jax.random.uniform(jax.random.fold_in(jax.random.fold_in(stream_key, 6), position), (parts,), jnp.float32, least / len(pieces), high / len(pieces))
        gain = gain * jnp.repeat(jnp.exp(steps), shape[position] // parts).reshape((-1,) + (1,) * (len(shape) - 1 - position))
    return gain


def length_profile(count, total, most, lean):
    portions = [(1 << 20) // math.isqrt(grade ** lean) + 1 for grade in range(2, count + 1)]
    surplus, given = total - most - (count - 1), [1] * (count - 1)
    while surplus > 0:
        free = [i for i in range(count - 1) if given[i] < most]
        mass, remaining = sum([portions[i] for i in free]), surplus
        for i in free:
            extra = min(most - given[i], max(1, remaining * portions[i] // mass), surplus)
            given[i] = given[i] + extra
            surplus = surplus - extra
    return np.array([most] + given)


def uneven_parts(key, number_of, total, most, lean):
    if number_of == 2:
        one = jax.random.randint(key, (), max(1, total - most), min(most, total - 1) + 1)
        return jnp.stack([one, total - one])
    tallies = jnp.asarray(length_profile(number_of, total, most, lean), jnp.int32)
    pairs = (number_of - 1) // 2
    donor, receiver = tallies[1:1 + 2 * pairs:2], tallies[2:2 + 2 * pairs:2]
    room = jnp.minimum(donor - 1, most - receiver)
    moved = jax.random.randint(jax.random.fold_in(key, 1), (pairs,), 0, 1 << 20) % (room + 1)
    tallies = tallies.at[1:1 + 2 * pairs:2].set(donor - moved).at[2:2 + 2 * pairs:2].set(receiver + moved)
    return tallies[jax.random.permutation(jax.random.fold_in(key, 2), number_of)]


def gaussian(stream_key, shape, scale, reach, cuts=(), kind=jnp.bfloat16):
    result = jax.random.normal(stream_key, shape, jnp.float32) * scale
    if len(cuts) > 0:
        result = shard_levels(stream_key, shape, cuts, -0.22, 0.18) * result
    return jnp.clip(result, min=-reach, max=reach).astype(kind)


def setup_inputs(seed: int = 0) -> dict:
    seeds = jax.random.split(jax.random.key(seed), 15)
    return {
        "tokens": gaussian(seeds[0], (TOKENS, D), 1.0, 6.0, ((0, 16),)),
        "lengths": jax.vmap(lambda own: uneven_parts(own, SEQS, NBLK, SPAN, 0))(jax.random.split(seeds[1], ROWS)).reshape((ROWS, SEQS)).astype(jnp.int32),
        "w_qkv": gaussian(seeds[2], (D, 3 * D), D ** -0.5, 0.25),
        "w_out": gaussian(seeds[3], (D, D), (D // 8) ** -0.5, 0.75),
        "w_sort": gaussian(seeds[4], (D, HEADS * SPAN), 5 ** -0.5, 2.5),
        "gain_attn": jnp.clip(1.0 + 0.1 * jax.random.normal(seeds[5], (D,), jnp.float32), 0.5, 1.5),
        "bias_attn": gaussian(seeds[6], (D,), 0.3, 1.5, (), jnp.float32),
        "gain_ffn": jnp.clip(1.0 + 0.1 * jax.random.normal(seeds[7], (D,), jnp.float32), 0.5, 1.5),
        "bias_ffn": gaussian(seeds[8], (D,), 0.3, 1.5, (), jnp.float32),
        "w_up": gaussian(seeds[9], (D, FF), D ** -0.5, 0.25),
        "bias_up": gaussian(seeds[10], (FF,), 0.3, 1.5, (), jnp.float32),
        "w_down": gaussian(seeds[11], (FF, D), FF ** -0.5, 0.125),
        "bias_down": gaussian(seeds[12], (D,), 0.3, 1.5, (), jnp.float32),
        "cotangent": gaussian(seeds[13], (TOKENS, D), 1.0, 6.0, ((0, 16),)),
    }


highest = lax.Precision.HIGHEST

@jax.custom_vjp
def coarse_arithmetic(v):
    return lax.optimization_barrier(v.astype(jnp.bfloat16)).astype(jnp.float32)

@jax.custom_vjp
def low_back(v):
    return v

def low_keep(v):
    return (coarse_arithmetic(v), None)

def low_pass(kept, grad):
    return (grad,)

def back_keep(v):
    return (v, None)

def back_low(kept, grad):
    return (coarse_arithmetic(grad),)
coarse_arithmetic.defvjp(low_keep, low_pass)
low_back.defvjp(back_keep, back_low)

def both_ways(value):
    return coarse_arithmetic(low_back(value))

def layer_norm(features, norm_gain, norm_shift):
    average = lax.optimization_barrier(jnp.mean(features, axis=-1, keepdims=True))
    centered = features - average
    variance = lax.optimization_barrier(jnp.mean(centered * centered, axis=-1, keepdims=True))
    return centered * lax.rsqrt(variance + 1e-05) * norm_gain + norm_shift

def block_layout(seq_lengths, block_count):
    seq_ends = jnp.cumsum(seq_lengths, dtype=jnp.int32)
    places = jnp.arange(block_count, dtype=jnp.int32)
    passed = places[:, None] >= seq_ends[None, :]
    owners = lax.optimization_barrier(jnp.sum(passed.astype(jnp.int32), axis=1, dtype=jnp.int32))
    first_block = lax.optimization_barrier(jnp.sum(jnp.where(passed, seq_lengths[None, :], 0), axis=1, dtype=jnp.int32))
    same_seq = owners[:, None] == owners[None, :]
    eligible_pattern = same_seq & (places[None, :] <= places[:, None])
    earlier_quantity = same_seq & (places[None, :] < places[:, None])
    offset = places[None, :] - first_block[:, None]
    columns = jnp.arange(SPAN, dtype=jnp.int32)
    onehot_lines = (offset[:, :, None] == columns[None, None, :]).astype(jnp.float32)
    opening = places == first_block
    return (eligible_pattern, earlier_quantity, onehot_lines, opening)

def attend_mask(opening):
    positions = jnp.arange(BLK, dtype=jnp.int32)
    causal = positions[None, :] <= positions[:, None]
    block_count = opening.shape[0]
    near_ok = jnp.broadcast_to(causal[None], (block_count, BLK, BLK))
    far_ok = jnp.broadcast_to(jnp.logical_not(opening)[:, None, None], (block_count, BLK, BLK))
    return jnp.concatenate([near_ok, far_ok], axis=2)[:, None]

def doubly_stochastic_balance(permutation_score_table, onehot_lines, eligible_pattern, earlier_quantity):
    placed = jnp.einsum('ihc,ijc->hij', permutation_score_table, onehot_lines, precision=highest)
    current = jnp.where(eligible_pattern[None], placed, -10000.0)
    for sweep in range(SINK):
        current = current - jax.nn.logsumexp(current, axis=2, keepdims=True)
        current = current - jax.nn.logsumexp(current, axis=1, keepdims=True)
    return jnp.where(earlier_quantity[None], jnp.exp(current), 0.0)

def attention_half(inputs, seq_lengths, w_qkv, w_out, w_sort, gain_attn, bias_attn):
    row_count = inputs.shape[0]
    block_count = row_count // BLK
    eligible_pattern, earlier_quantity, onehot_lines, opening = block_layout(seq_lengths, block_count)
    normed = layer_norm(inputs, gain_attn, bias_attn)
    packed = jnp.dot(coarse_arithmetic(normed), w_qkv, precision=highest)
    queries = both_ways(packed[:, :D]).reshape(block_count, BLK, HEADS, HDIM)
    keys_near = both_ways(packed[:, D:2 * D]).reshape(block_count, BLK, HEADS, HDIM)
    values_near = both_ways(packed[:, 2 * D:]).reshape(block_count, BLK, HEADS, HDIM)
    summary = coarse_arithmetic(lax.optimization_barrier(jnp.mean(normed.reshape(block_count, BLK, D), axis=1)))
    segment_scores_raw = low_back(jnp.dot(summary, w_sort, precision=highest)).reshape(block_count, HEADS, SPAN)
    segment_blend = coarse_arithmetic(doubly_stochastic_balance(segment_scores_raw, onehot_lines, eligible_pattern, earlier_quantity))
    keys_far = both_ways(jnp.einsum('hij,jthd->ithd', segment_blend, keys_near, precision=highest))
    values_far = both_ways(jnp.einsum('hij,jthd->ithd', segment_blend, values_near, precision=highest))
    keys_all = jnp.concatenate([keys_near, keys_far], axis=1)
    values_all = jnp.concatenate([values_near, values_far], axis=1)
    score_scale = 1.0 / math.sqrt(HDIM)
    scores = low_back(jnp.einsum('ithd,ishd->ihts', queries, keys_all, precision=highest) * score_scale)
    scores = jnp.where(attend_mask(opening), scores, -1000000000.0)
    soft_low = coarse_arithmetic(jax.nn.softmax(scores, axis=-1))
    attended = jnp.einsum('ihts,ishd->ithd', soft_low, values_all, precision=highest)
    attended = both_ways(attended.reshape(row_count, D))
    return both_ways(inputs + jnp.dot(attended, w_out, precision=highest))

def ffn_half(middle, gain_ffn, bias_ffn, w_up, bias_up, w_down, bias_down):
    normed = layer_norm(middle, gain_ffn, bias_ffn)
    hidden_pre = low_back(jnp.dot(coarse_arithmetic(normed), w_up, precision=highest) + bias_up)
    active = coarse_arithmetic(jax.nn.gelu(hidden_pre))
    return middle + jnp.dot(active, w_down, precision=highest) + bias_down

def reference(tokens, lengths, w_qkv, w_out, w_sort, gain_attn, bias_attn, gain_ffn, bias_ffn, w_up, bias_up, w_down, bias_down, cotangent):
    weights = tuple((member.astype(jnp.float32) for member in (w_qkv, w_out, w_sort, gain_attn, bias_attn, gain_ffn, bias_ffn, w_up, bias_up, w_down, bias_down)))
    inputs = tokens.astype(jnp.float32).reshape(ROWS, MB, D)

    def forward(inputs, weights):

        def one_batch(packet):
            rows_in, seq_lengths = packet
            middle = attention_half(rows_in, seq_lengths, *weights[:5])
            return ffn_half(middle, *weights[5:])
        return lax.map(jax.checkpoint(one_batch), (inputs, lengths))
    outputs, pullback = jax.vjp(forward, inputs, weights)
    grad_in, grads = pullback(cotangent.astype(jnp.float32).reshape(ROWS, MB, D))
    ends = jnp.stack([grad_in.reshape(TOKENS, D), outputs.reshape(TOKENS, D)])
    return (ends, grads[0], grads[1], grads[2], grads[3], grads[4], grads[5], grads[6], grads[7], grads[8], grads[9], grads[10])
```

```python
import functools
import math

import jax
import jax.numpy as jnp
from jax import lax
from jax.experimental import pallas as pl
from jax.experimental.pallas import tpu as pltpu
from jax.sharding import PartitionSpec as P

D = 512
HEADS = 8
HDIM = 64
FF = 2048
BLK = 32
SINK = 8
SPAN = 32
T = 2048
NB = T // BLK
TA = 256
TF = 512
FC = 512
GL = 256
GOUT, GQ0, GQ1 = 16384, 18432, 21504
PIECE = 512
GAP = BLK + 1
SCALE = 1.0 / math.sqrt(HDIM)
BF = jnp.bfloat16
F32 = jnp.float32


def dot(a, b):
    return jnp.dot(a, b, preferred_element_type=F32)


def dot_nt(a, b):
    return lax.dot_general(a, b, (((1,), (1,)), ((), ())), preferred_element_type=F32)


def iota(shape, axis):
    return lax.broadcasted_iota(jnp.int32, shape, axis)


def normalise(x):
    xc = x - jnp.mean(x, axis=-1, keepdims=True)
    rstd = lax.rsqrt(jnp.mean(xc * xc, axis=-1, keepdims=True) + 1e-5)
    return xc * rstd, rstd


def normalise_back(g, xhat, rstd, gain):
    gg = g * gain
    return rstd * (
        gg
        - jnp.mean(gg, axis=-1, keepdims=True)
        - xhat * jnp.mean(gg * xhat, axis=-1, keepdims=True)
    )


def spread_heads(x, low, high):
    a, b = x[:, :128], x[:, 128:]
    z = jnp.zeros_like(a)
    rows = ([a * low, z], [a * high, z], [z, b * low], [z, b * high])
    return jnp.concatenate([jnp.concatenate(r, axis=1) for r in rows], axis=0)


def take_heads(x, first):
    r = x.shape[0] // 4
    tiles = [
        jnp.where(first, x[2 * c * r : (2 * c + 1) * r, c * 128 : (c + 1) * 128],
                  x[(2 * c + 1) * r : (2 * c + 2) * r, c * 128 : (c + 1) * 128])
        for c in range(2)
    ]
    return jnp.concatenate(tiles, axis=1)


def spread_even(x, low, high):
    a, b = x[:, :128], x[:, 128:]
    rows = ([a * low, b * low], [a * high, b * high])
    return jnp.concatenate([jnp.concatenate(r, axis=1) for r in rows], axis=0)


def spread_pair(x):
    z = jnp.zeros_like(x[:, :128])
    rows = ([x[:, :128], z], [z, x[:, 128:]])
    return jnp.concatenate([jnp.concatenate(r, axis=1) for r in rows], axis=0)


def beside(ref, count, rows):
    return jnp.concatenate([ref[n * rows : (n + 1) * rows] for n in range(count)], axis=1)


def settle(x):
    y = x.reshape(2, NB, 2 * NB)
    y = y - jnp.max(y, axis=1, keepdims=True)
    ex = jnp.exp(y)
    tot = jnp.sum(ex, axis=1, keepdims=True)
    return (ex * inverse(tot)).reshape(x.shape), (y - jnp.log(tot)).reshape(x.shape)


def settle_back(g, p):
    tot = jnp.sum(g.reshape(2, NB, 2 * NB), axis=1, keepdims=True)
    return g - (p.reshape(2, NB, 2 * NB) * tot).reshape(g.shape)


def wide(acc, rows, lanes=range(D // 128)):
    return jnp.concatenate([acc[c, rows] for c in lanes], axis=1)


def put_wide(acc, rows, value):
    for c in range(value.shape[1] // 128):
        acc[c, rows] = value[:, c * 128 : (c + 1) * 128]


def add_wide(acc, rows, value):
    for c in range(value.shape[1] // 128):
        acc[c, rows] += value[:, c * 128 : (c + 1) * 128]


def block_rows(block):
    return pl.ds(block * GAP, BLK)


def get_blocks(acc, first, count, lanes=range(D // 128)):
    return jnp.concatenate([wide(acc, block_rows(first + n), lanes) for n in range(count)], axis=0)


def put_blocks(acc, first, value, lane=0):
    for n in range(value.shape[0] // BLK):
        for c in range(value.shape[1] // 128):
            part = value[n * BLK : (n + 1) * BLK, c * 128 : (c + 1) * 128]
            acc[lane + c, block_rows(first + n)] = part


def flat_rows(ref, base, step, count):
    parts = [ref[pl.ds(pl.multiple_of(base + c * step, 16), count)] for c in range(D // 128)]
    return jnp.concatenate(parts, axis=1)


def put_flat(ref, base, value):
    rows = value.shape[0]
    for c in range(value.shape[1] // 128):
        ref[pl.ds(pl.multiple_of(base + c * rows, 16), rows)] = value[:, c * 128 : (c + 1) * 128]


def inverse(x):
    r = pl.reciprocal(x, approx=True)
    return r * (2.0 - x * r)


def gelu_both(u):
    c = math.sqrt(2.0 / math.pi)
    e = -2.0 * c / math.log(2.0)
    u2 = u * u
    power = jnp.minimum(u * (e + (e * 0.044715) * u2), 120.0)
    half = pl.reciprocal(1.0 + jnp.exp2(power), approx=True)
    act = u * half
    slope = half + act * (1.0 - half) * (2.0 * c + (6.0 * c * 0.044715) * u2)
    return act, slope


AXES = {16: ((1, 2), (2, 2), (4, 4)), 128: ((1, 4), (32, 4), (4, 8))}


def axes_of(dp):
    if dp in AXES:
        return AXES[dp]
    a = max(n for n in range(1, dp + 1) if dp % (n * n) == 0)
    return (1, a), (a, a), (a * a, dp // (a * a))


class Links:
    def __init__(self, groups):
        self.sec, self.dp = lax.axis_index("section"), lax.axis_index("dp")
        self.levels = []
        for axes in groups:
            own = [lax.rem(lax.div(self.dp, stride), n) for stride, n in axes]
            me, scale = 0, 1
            for (_, n), at in zip(axes, own):
                me, scale = me + at * scale, scale * n
            self.levels.append((axes, own, me))
        self.sizes = [2] + [math.prod(n for _, n in axes) for axes in groups]
        self.first = [0]
        for n in self.sizes:
            self.first.append(self.first[-1] + n - 1)
        self.copies = self.first[-1]

    def place(self, level, k):
        return lax.rem(self.levels[level - 1][2] + k, self.sizes[level])

    def peer(self, level, k):
        if level == 0:
            return (1 - self.sec, self.dp)
        axes, own, _ = self.levels[level - 1]
        place, to = self.place(level, k), self.dp
        for (stride, n), at in zip(axes, own):
            to = to + (lax.rem(place, n) - at) * stride
            place = lax.div(place, n)
        return (self.sec, to)

    def everyone(self):
        return [
            self.peer(level, k)
            for level in range(len(self.sizes))
            for k in range(1, self.sizes[level])
        ]


def all_links(dp):
    a, b, c = axes_of(dp)
    sec = lax.axis_index("section")
    a1 = (a[0] + sec * (b[0] - a[0]), a[1])
    b1 = (b[0] + sec * (a[0] - b[0]), b[1])
    return Links([[a1], [b1], [c]]), Links([[a, b], [c]])


def copies_of(dp):
    a, b, c = axes_of(dp)
    return a[1] * b[1] + c[1] - 1


def remote(src, dst, ssem, rsem, device):
    return pltpu.make_async_remote_copy(
        src_ref=src,
        dst_ref=dst,
        send_sem=ssem,
        recv_sem=rsem,
        device_id=device,
        device_id_type=pl.DeviceIdType.MESH,
    )


class Packet:
    def __init__(self, links, ref, out, base, rows, inboxes, ssem, rsem, osem, number):
        self.links, self.ref, self.out, self.inboxes = links, ref, out, inboxes
        self.ssem, self.rsem, self.osem, self.number = ssem, rsem, osem, number
        self.deep = len(links.sizes)
        self.last = 2 * self.deep
        half = rows // 2
        self.size = [half]
        self.off = [base + links.sec * half]
        self.away = base + (1 - links.sec) * half
        self.inpos = [0, 0 if inboxes[0] is not inboxes[1] else half]
        for level in range(1, self.deep):
            n = links.sizes[level]
            self.size.append(self.size[-1] // n)
            self.off.append(self.off[-1] + links.place(level, 0) * self.size[-1])
            self.inpos.append(self.inpos[-1] + (n - 1) * self.size[-1])

    def rows(self, ref, off, level):
        return ref.at[pl.ds(pl.multiple_of(off, 16), self.size[level])]

    def landing(self, level, k, skip, count):
        box, base = self.inboxes[min(level, 1)]
        at = base + self.inpos[level] + (k - 1) * self.size[level] + skip
        return box, pl.ds(pl.multiple_of(at, 16), count)

    def pieces(self, level):
        count = -(-self.size[level] // PIECE)
        rows = self.size[level] // count
        return [(n * rows, rows) for n in range(count)]

    def reduce_start(self, level, k):
        off = self.away
        if level > 0:
            off = self.off[level - 1] + self.links.place(level, k) * self.size[level]
        for skip, count in self.pieces(level):
            box, rows = self.landing(level, k, skip, count)
            remote(
                self.ref.at[pl.ds(pl.multiple_of(off + skip, 16), count)],
                box.at[rows],
                self.ssem.at[self.number],
                self.rsem.at[self.number, level],
                self.links.peer(level, k),
            ).start()

    def gather_start(self, level, k):
        source = self.ref if level == self.deep - 1 else self.out
        for skip, count in self.pieces(level):
            rows = pl.ds(pl.multiple_of(self.off[level] + skip, 16), count)
            remote(
                source.at[rows],
                self.out.at[rows],
                self.ssem.at[self.number],
                self.rsem.at[self.number, self.deep + level],
                self.links.peer(level, k),
            ).start()

    def arrived(self, level, gathered):
        count = (self.links.sizes[level] - 1) * self.size[level]
        if count == 0:
            return
        if not gathered:
            box, rows = self.landing(level, 1, 0, count)
            what = box.at[rows]
        else:
            base = self.away if level == 0 else self.off[level - 1]
            what = self.out.at[pl.ds(pl.multiple_of(base, 16), count)]
        sem = self.rsem.at[self.number, level + (self.deep if gathered else 0)]
        remote(what, what, self.ssem.at[self.number], sem, self.links.peer(0, 1)).wait_recv()

    def sent(self, source):
        count = 2 * sum((n - 1) * size for n, size in zip(self.links.sizes, self.size))
        what = source.at[pl.ds(0, count)]
        sem = self.rsem.at[self.number, 0]
        remote(what, what, self.ssem.at[self.number], sem, self.links.peer(0, 1)).wait_send()

    def own_copy(self):
        return pltpu.make_async_copy(
            self.rows(self.ref, self.off[-1], -1),
            self.rows(self.out, self.off[-1], -1),
            self.osem.at[self.number],
        )

    def ks(self, level):
        return range(1, self.links.sizes[level])

    def add(self, level):
        size = self.size[level]
        chunk = size // -(-size // 1024)
        wide_sum = self.links.sizes[level] > 2

        @pl.loop(0, size // chunk)
        def _(j):
            rows = pl.ds(pl.multiple_of(self.off[level] + j * chunk, 16), chunk)
            total = self.ref[rows]
            if wide_sum:
                total = total.astype(F32)
            for k in self.ks(level):
                box, came = self.landing(level, k, j * chunk, chunk)
                total += box[came].astype(total.dtype)
            self.ref[rows] = total.astype(BF)

    def step(self, n):
        deep = self.deep
        if 1 <= n <= deep:
            self.arrived(n - 1, False)
            self.add(n - 1)
        if n == deep:
            self.own_copy().start()
        if n == deep + 1:
            self.own_copy().wait()
        if n > deep:
            self.arrived(self.last - n, True)
        if n < deep:
            for k in self.ks(n):
                self.reduce_start(n, k)
        elif n < self.last:
            for k in self.ks(self.last - 1 - n):
                self.gather_start(self.last - 1 - n, k)


PLAN = {
    ("ffnend", 0): (("f0", 0),),
    ("ffn", 1, 2): (("f0", 1),),
    ("ffnend", 1): (("f1", 0),),
    ("ffn", 2, 2): (("f1", 1), ("f0", 2),),
    ("ffnend", 2): (("f2", 0),),
    ("ffn", 3, 1): (("f1", 2),),
    ("ffn", 3, 2): (("f2", 1), ("f0", 3),),
    ("ffnend", 3): (("f1", 3), ("f3", 0),),
    ("six", 3): (("f2", 2),),
    ("six", 4): (("f3", 1),),
    ("six", 6): (("f0", 4),),
    ("sixend",): (("o", 0), ("vf", 0),),
    ("seven", 0, 2): (("f1", 4),),
    ("seven", 0, 3): (("f2", 3), ("o", 1), ("vf", 1),),
    ("seven", 0, 4): (("f3", 2),),
    ("seven", 0, 7): (("f0", 5),),
    ("eight", 0, 0): (("o", 2),),
    ("eight", 0, 1): (("vf", 2),),
    ("eight", 0, 3): (("f3", 3),),
    ("eight", 0, 4): (("f1", 5),),
    ("eight", 0, 6): (("f0", 6),),
    ("nine", 0): (("vf", 3), ("q0", 0),),
    ("seven", 1, 0): (("f2", 4), ("f1", 6),),
    ("seven", 1, 1): (("o", 3),),
    ("seven", 1, 2): (("q0", 1),),
    ("seven", 1, 3): (("f3", 4), ("f0", 7),),
    ("sevenend", 1): (("qa", 0),),
    ("eight", 1, 0): (("f1", 7),),
    ("eight", 1, 1): (("f0", 8),),
    ("eight", 1, 2): (("f2", 5),),
    ("eight", 1, 3): (("q0", 2),),
    ("nine", 1): (("o", 4), ("qv", 0),),
    ("eight", 2, 0): (("qa", 1), ("f1", 8),),
    ("eight", 2, 1): (("f2", 6),),
    ("eight", 2, 2): (("qv", 1), ("f3", 5),),
    ("eight", 2, 3): (("q0", 3),),
    ("nine", 2): (("qk", 0),),
    ("ten",): (("qa", 2), ("o", 5), ("qk", 1), ("z2", 0),),
    ("eleven", 0): (("f2", 7),),
    ("eleven", 1): (("q0", 4),),
    ("eleven", 2): (("qv", 2), ("z2", 1), ("f3", 6),),
    ("eleven", 3): (("qa", 3), ("o", 6), ("f2", 8),),
    ("eleven", 4): (("qk", 2),),
    ("eleven", 6): (("z2", 2),),
    ("eleven", 7): (("q0", 5), ("qv", 3),),
    ("tail",): (
        ("va", 0), ("qa", 4), ("f3", 7), ("qk", 3), ("va", 1), ("o", 7), ("z2", 3), ("q0", 6),
        ("f3", 8), ("qv", 4), ("o", 8), ("va", 2), ("qa", 5), ("qk", 4), ("z2", 4), ("q0", 7),
        ("qa", 6), ("va", 3), ("qv", 5), ("q0", 8), ("qk", 5), ("qv", 6), ("z2", 5), ("qk", 6),
        ("z2", 6),
    ),
}


def kernel(
    dp,
    len_ref,
    tok_ref,
    cot_ref,
    wqkv_ref,
    wout,
    wsort,
    gain_a_ref,
    bias_a_ref,
    gain_f_ref,
    bias_f_ref,
    bias_d_ref,
    wup,
    bup,
    wdown,
    ends_o,
    grads_o,
    sort_o,
    vec_o,
    xs,
    wqkv,
    w1,
    w2,
    cs,
    qs,
    ks,
    vs,
    kts,
    vts,
    kfs,
    vfs,
    ps,
    attt,
    mid,
    nf,
    nft,
    cott,
    acc0,
    acc1,
    mcat,
    mcatt,
    psave,
    summ,
    gm,
    halves,
    actb,
    gpreb,
    gr,
    gz,
    vb,
    vin,
    sem_in,
    ssem,
    rsem,
    out_sem,
    end_send,
    end_recv,
):
    deep, flat = all_links(dp)
    sec = deep.sec
    mine = pl.ds(pl.multiple_of(sec * T, T), T)
    for c in range(4):
        lanes = slice(c * 128, (c + 1) * 128)
        pltpu.make_async_copy(
            tok_ref.at[mine, lanes], xs.at[pl.ds(c * T, T)], sem_in.at[0]
        ).start()
    e0 = len_ref[sec, 0]
    e1 = e0 + len_ref[sec, 1]
    gain_a, bias_a = gain_a_ref[...], bias_a_ref[...]
    gain_f, bias_f = gain_f_ref[...], bias_f_ref[...]
    bias_d = bias_d_ref[...]
    vb[...] = jnp.zeros_like(vb)
    w_copy = pltpu.make_async_copy(wqkv_ref, wqkv, sem_in.at[4])
    w_copy.start()
    x_part = xs.at[pl.ds(0, 4 * T)]
    pltpu.make_async_copy(x_part, x_part, sem_in.at[0]).wait()
    w_copy.wait()
    cot_copy = pltpu.make_async_copy(cot_ref.at[mine], cs, sem_in.at[1])
    cot_copy.start()
    for c in range(FF // FC):
        for l in range(4):
            to = pl.ds((c * 4 + l) * FC, FC)
            lane = l * 128
            pltpu.make_async_copy(
                wup.at[:, pl.ds(c * FC + lane, 128)], w1.at[to], sem_in.at[2]
            ).start()
            pltpu.make_async_copy(
                wdown.at[pl.ds(c * FC, FC), pl.ds(lane, 128)], w2.at[to], sem_in.at[3]
            ).start()

    def packet(number, base, rows, links, box, more=None, ref=gr, out=grads_o):
        boxes = (box, box if more is None else more)
        return Packet(links, ref, out, base, rows, boxes, ssem, rsem, out_sem, number)

    boxes = ((xs, 0), (xs, 4096), (w1, 0), (w2, 0))
    f = [packet(p, p * 4096, 4096, deep, boxes[p]) for p in range(4)]
    parts = dict(f0=f[0], f1=f[1], f2=f[2], f3=f[3])
    if 1024 % (32 * dp) == 0:
        parts["o"] = packet(4, GOUT, 2048, deep, (w1, 4096))
        parts["q0"] = packet(5, GQ0, 3072, deep, (w2, 4096))
        parts["qa"] = packet(6, GQ1, 1024, flat, (w1, 6144))
        parts["qk"] = packet(7, GQ1 + 1024, 1024, flat, (w1, 0))
        parts["qv"] = packet(8, GQ1 + 2048, 1024, flat, (w1, 1024))
        parts["z2"] = packet(9, 0, 1024, flat, (w2, 7168), ref=gz, out=sort_o)
    else:
        parts["qk"] = packet(4, GOUT, 8192, flat, (w1, 0))
        parts["z2"] = packet(5, 0, gz.shape[0], flat, (w2, 4096), ref=gz, out=sort_o)

    class Vectors:
        def __init__(self, number, base):
            self.number, self.rows = number, pl.ds(base, 8)

        def copy(self, level, k):
            at = flat.first[level] + k - 1
            return remote(
                vb.at[self.rows],
                vin.at[at, self.rows],
                ssem.at[self.number],
                rsem.at[self.number, level],
                flat.peer(level, k),
            )

        def step(self, n):
            if n >= 1:
                first, count = flat.first[n - 1], flat.sizes[n - 1] - 1
                if count:
                    came = vin.at[pl.ds(first, count), self.rows]
                    sem = rsem.at[self.number, n - 1]
                    both = remote(came, came, ssem.at[self.number], sem, flat.peer(0, 1))
                    both.wait_send()
                    both.wait_recv()
                for k in range(count):
                    vb[self.rows] += vin[first + k, self.rows]
            if n < len(flat.sizes):
                for k in range(1, flat.sizes[n]):
                    self.copy(n, k).start()

    packets = list(parts.values())
    parts["vf"] = Vectors(10, 0)
    parts["va"] = Vectors(11, 8)
    def steps(*where):
        for name, n in PLAN.get(where, ()):
            if name in parts:
                parts[name].step(n)

    def steps_at(i, *where):
        for place in PLAN:
            if place[:-1] == where:

                @pl.when(i == place[-1])
                def _():
                    steps(*place)

    def end_copies(at, count, far_sec, staged):
        tile = staged.at[pl.ds(pl.multiple_of(at, TA), count)]
        there = ends_o.at[pl.ds(pl.multiple_of(sec * T + at, TA), count)]
        away = remote(tile, there, end_send.at[far_sec], end_recv.at[0], flat.peer(0, 1))
        return away, pltpu.make_async_copy(tile, there, end_send.at[far_sec])

    def put_end(i, far_sec, staged):
        away, here = end_copies(i * TA, TA, far_sec, staged)

        @pl.when(sec == far_sec)
        def _():
            away.start()

        @pl.when(sec != far_sec)
        def _():
            here.start()

    def wait_end(far_sec, staged):
        away, here = end_copies(0, T, far_sec, staged)

        @pl.when(sec == far_sec)
        def _():
            away.wait_send()

        @pl.when(sec != far_sec)
        def _():
            here.wait()

    lane = iota((NB, 128), 1)
    halves[0] = (lane < HDIM).astype(BF)
    halves[1] = (lane >= HDIM).astype(BF)

    @pl.loop(0, T // TA)
    def _(i):
        rows = pl.ds(pl.multiple_of(i * TA, TA), TA)
        xhat, _ = normalise(flat_rows(xs, i * TA, T, TA).astype(F32))
        normed = xhat * gain_a + bias_a
        low = normed.astype(BF)
        packed = dot(low, wqkv[...]).astype(BF)
        qs[rows] = packed[:, :D]
        k, v = packed[:, D : 2 * D], packed[:, 2 * D :]
        ks[rows] = k
        vs[rows] = v
        nb = TA // BLK
        put_blocks(acc0, i * nb, k.astype(F32))
        put_blocks(acc1, i * nb, v.astype(F32))
        summ[pl.ds(pl.multiple_of(i * nb, nb), nb)] = jnp.mean(
            normed.reshape(nb, BLK, D), axis=1
        )

    blk = iota((2 * NB, 2 * NB), 0) & (NB - 1)
    col = iota((2 * NB, 2 * NB), 1) & (NB - 1)
    owner = (blk >= e0).astype(jnp.int32) + (blk >= e1).astype(jnp.int32)
    col_owner = (col >= e0).astype(jnp.int32) + (col >= e1).astype(jnp.int32)
    same = owner == col_owner
    allowed = same & (col <= blk)
    before = same & (col < blk)
    a = iota((HEADS * SPAN, D), 0)
    b = iota((HEADS * SPAN, D), 1)
    gap = jnp.where(a >> 5 == b >> 6, (b & (HDIM - 1)) - (a & (SPAN - 1)), -1000)
    row = iota((NB, D), 0)
    firsts = (jnp.int32(0), e0, e1)
    lasts = (e0, e1, jnp.int32(NB))
    logits = dot(summ[...].astype(BF), wsort[...])
    high = logits.astype(BF)
    rest = logits - high.astype(F32)
    middle = rest.astype(BF)
    three = jnp.concatenate([high, middle, (rest - middle.astype(F32)).astype(BF)], axis=0)
    placed = jnp.zeros((NB, D), F32)
    for s in range(3):
        moved = dot(three, (gap == firsts[s]).astype(BF))
        moved = moved[:NB] + moved[NB : 2 * NB] + moved[2 * NB :]
        placed = jnp.where(row >= firsts[s], moved, placed)
    start = []
    for g in range(2):
        tiles = [placed[:, c : c + 128] for c in (2 * g * 128, (2 * g + 1) * 128)]
        start.append(jnp.where(allowed, jnp.concatenate(tiles, axis=0), -10000.0))

    def sweep(it, cur):
        for n in range(2):
            cur = [x.T for x in cur]
            done = [settle(x) for x in cur]
            for g in range(2):
                psave[2 * it + n, g] = done[g][0]
            cur = [x for _, x in done]
        return tuple(cur)

    lax.fori_loop(0, SINK, sweep, tuple(start))
    for g in range(2):
        mix = jnp.where(before, psave[2 * SINK - 1, g], 0.0)
        mcat[g] = mix.astype(BF)
        for p in range(2):
            tr = mix[p * NB : (p + 1) * NB].T.astype(BF)
            mcatt[g, p * NB : (p + 1) * NB] = jnp.concatenate([tr[:NB], tr[NB:]], axis=1)

    @pl.loop(0, BLK // 4)
    def _(it):
        low, high = halves[0], halves[1]
        jobs, outs = [], []
        for u in range(4):
            t = it * 4 + u
            every = pl.ds(t, NB, stride=GAP)
            for acc, keep in ((acc0, kts), (acc1, vts)):
                x = wide(acc, every).astype(BF)
                keep[pl.ds(pl.multiple_of(t * NB, NB), NB)] = x
                jobs.append((acc, every, x))
        for acc, every, x in jobs:
            for g in range(2):
                far = dot(mcat[g], spread_even(x[:, g * GL : (g + 1) * GL], low, high))
                outs.append((acc, every, g, far))
        for acc, every, g, far in outs:
            acc[2 * g, every] = far[:NB, :128].astype(BF).astype(F32)
            acc[2 * g + 1, every] = far[NB:, 128:].astype(BF).astype(F32)

    pair = 2 * BLK
    srow = iota((2 * pair, GL), 0)
    tcol = iota((2 * pair, GL), 1) & (pair - 1)
    together = (srow & BLK) == (tcol & BLK)
    own_ok = together & (srow < pair) & ((srow & (BLK - 1)) <= (tcol & (BLK - 1)))
    far_ok = together & (srow >= pair)

    cot_copy.wait()

    @pl.loop(0, T // TA)
    def _(i):
        low, high = halves[0], halves[1]
        first = iota((pair, 128), 1) < HDIM
        seen, scores = [], []
        for j in range(TA // pair):
            block = (i * (TA // pair) + j) * 2
            rows = pl.ds(pl.multiple_of(block * BLK, pair), pair)
            kf = get_blocks(acc0, block, 2).astype(BF)
            vf16 = get_blocks(acc1, block, 2).astype(BF)
            kfs[rows] = kf
            vfs[rows] = vf16
            kseen = jnp.concatenate([ks[rows], kf], axis=0)
            seen.append(jnp.concatenate([vs[rows], vf16], axis=0))
            q = qs[rows] * SCALE
            closed = []
            for n in (block, block + 1):
                opening = (n == 0) | (n == e0) | (n == e1)
                closed.append(jnp.where(opening, 0, 1))
            open_far = jnp.where(tcol < BLK, closed[0], closed[1]) == 1
            valid = own_ok | (far_ok & open_far)
            for g in range(2):
                lanes = slice(g * GL, (g + 1) * GL)
                sc = dot_nt(kseen[:, lanes], spread_heads(q[:, lanes], low, high))
                scores.append(jnp.where(valid, sc, -1e9))
        sc = jnp.concatenate(scores, axis=1)
        ex = jnp.exp(sc - jnp.max(sc, axis=0, keepdims=True))
        w16 = (ex * inverse(jnp.sum(ex, axis=0, keepdims=True))).astype(BF)
        ws = [w16[:, c : c + GL] for c in range(0, w16.shape[1], GL)]
        turned = [w.T for w in ws]
        for n, w in enumerate(ws):
            prow = pl.ds(pl.multiple_of((i * (TA // pair) + n // 2) * pair, pair), pair)
            kept = [w[c : c + BLK] + w[c + BLK : c + pair] for c in (0, pair)]
            ps[prow, n % 2 * GL : (n % 2 + 1) * GL] = jnp.concatenate(kept, axis=0)
        products = [
            dot(w, seen[n // 2][:, n % 2 * GL : (n % 2 + 1) * GL]) for n, w in enumerate(turned)
        ]
        made = [take_heads(r, first).astype(BF) for r in products]
        rows = pl.ds(pl.multiple_of(i * TA, TA), TA)
        att = jnp.concatenate(
            [jnp.concatenate(made[n : n + 2], axis=1) for n in range(0, len(made), 2)], axis=0
        )
        for n in range(2):
            at = pl.multiple_of(i * D + n * TA, TA)
            attt[pl.ds(at, TA)] = att[:, n * TA : (n + 1) * TA]
        x = flat_rows(xs, i * TA, T, TA).astype(F32)
        middle = (x + dot(att, wout[...])).astype(BF)
        mid[rows] = middle
        xhat, _ = normalise(middle.astype(F32))
        nf[rows] = (xhat * gain_f + bias_f).astype(BF)

    barrier = pltpu.get_barrier_semaphore()
    everyone = flat.everyone()
    for device in everyone:
        pl.semaphore_signal(
            barrier, inc=1, device_id=device, device_id_type=pl.DeviceIdType.MESH
        )

    @pl.loop(0, T // TF)
    def _(i):
        rows = pl.ds(pl.multiple_of(i * TF, TF), TF)
        nft[rows] = nf[rows].T
        cott[rows] = cs[rows].T
        put_wide(acc0, rows, jnp.zeros((TF, D), F32))
        put_wide(acc1, rows, jnp.zeros((TF, D), F32))

    pltpu.make_async_copy(w1, w1, sem_in.at[2]).wait()
    pltpu.make_async_copy(w2, w2, sem_in.at[3]).wait()
    pl.semaphore_wait(barrier, len(everyone))

    @pl.loop(0, FF // FC)
    def _(c):
        cols = pl.ds(pl.multiple_of(c * FC, FC), FC)
        @pl.loop(0, T // TF)
        def _(i):
            rows = pl.ds(pl.multiple_of(i * TF, TF), TF)
            up = flat_rows(w1, c * 4 * FC, FC, FC)
            down = flat_rows(w2, c * 4 * FC, FC, FC)
            pre = dot(nf[rows], up) + bup[0:1, cols]
            act, slope = gelu_both(pre)
            act = act.astype(BF)
            gact = dot_nt(cs[rows], down)
            gpre = slope * gact
            vb[pl.ds(4 + c, 1)] += jnp.sum(gpre, axis=0, keepdims=True)
            gpre = gpre.astype(BF)
            add_wide(acc0, rows, dot(act, down))
            add_wide(acc1, rows, dot_nt(gpre, up))
            actb[rows] = act
            gpreb[rows] = gpre
            for chunk in range(FF // FC):

                @pl.when(c == chunk)
                def _():
                    steps_at(i, "ffn", chunk)

        gu = dot(beside(nft, T // TF, D), gpreb[...])
        put_flat(gr, c * 4096, gu.astype(BF))
        gd = dot(beside(cott, T // TF, D), actb[...])
        put_flat(gr, c * 4096 + 2048, gd.T.astype(BF))

        steps_at(c, "ffnend")


    @pl.loop(0, T // TA)
    def _(i):
        rows = pl.ds(pl.multiple_of(i * TA, TA), TA)
        mf = mid[rows].astype(F32)
        gpreb[rows] = (mf + wide(acc0, rows) + bias_d).astype(BF)
        put_end(i, 0, gpreb)
        cot = cs[rows].astype(F32)
        gn = wide(acc1, rows)
        xhat, rstd = normalise(mf)
        vb[0:1] += jnp.sum(gn * xhat, axis=0, keepdims=True)
        vb[1:2] += jnp.sum(gn, axis=0, keepdims=True)
        vb[2:3] += jnp.sum(cot, axis=0, keepdims=True)
        nf[rows] = (cot + normalise_back(gn, xhat, rstd, gain_f)).astype(BF)
        steps_at(i, "six")

    x_copy = pltpu.make_async_copy(tok_ref.at[mine], cs, sem_in.at[0])
    x_copy.start()
    for n in range(T // TA):
        tile = [attt[n * D + m * TA : n * D + (m + 1) * TA] for m in range(2)]
        attt[n * D : (n + 1) * D] = jnp.concatenate(tile, axis=1).T
    gout = dot(beside(attt, T // TA, D), nf[...]).astype(BF)
    put_flat(gr, GOUT, gout)
    gm[...] = jnp.zeros_like(gm)
    steps("sixend")
    x_copy.wait()

    for g in range(2):
        lanes = slice(g * GL, (g + 1) * GL)
        base = (GQ0, GQ1)[g]

        @pl.loop(0, T // TA)
        def _(i):
            rows_t = pl.ds(pl.multiple_of(i * TA, TA), TA)
            gat = dot_nt(nf[rows_t], wout[lanes]).astype(BF)
            low, high = halves[0], halves[1]
            first = iota((pair, 128), 1) < HDIM
            block0 = (iota((BLK, GL), 1) & BLK == 0).astype(BF)
            block1 = (iota((BLK, GL), 1) & BLK != 0).astype(BF)
            blocks, spread, gws, w16s = [], [], [], []
            for j in range(TA // pair):
                at = pl.multiple_of((i * (TA // pair) + j) * pair, pair)
                rows = pl.ds(at, pair)
                vseen = jnp.concatenate([vs[rows, lanes], vfs[rows, lanes]], axis=0)
                gad = spread_heads(gat[j * pair : (j + 1) * pair], low, high)
                gws.append(dot_nt(vseen, gad))
                kept = ps[rows, lanes]
                own, far = kept[:BLK], kept[BLK:]
                w16s.append(
                    jnp.concatenate(
                        [own * block0, own * block1, far * block0, far * block1], axis=0
                    )
                )
                blocks.append(rows)
                spread.append(gad)
            w16 = jnp.concatenate(w16s, axis=1)
            gw = jnp.concatenate(gws, axis=1)
            w = w16.astype(F32)
            gs = w * (gw - jnp.sum(gw * w, axis=0, keepdims=True))
            gs = (gs * SCALE).astype(BF)
            gss = [gs[:, c : c + GL] for c in range(0, gs.shape[1], GL)]
            turned = [part.T for part in gss]
            gvs = [dot(w, gad).astype(BF) for w, gad in zip(w16s, spread)]
            gks = [
                dot(part, spread_heads(qs[rows, lanes], low, high)).astype(BF)
                for part, rows in zip(gss, blocks)
            ]
            gqs = []
            for part, rows in zip(turned, blocks):
                kseen = jnp.concatenate([ks[rows, lanes], kfs[rows, lanes]], axis=0)
                gqs.append(dot(part, kseen))
            for j, (rows, gk, gv, gq) in enumerate(zip(blocks, gks, gvs, gqs)):
                block = (i * (TA // pair) + j) * 2
                cott[rows, lanes] = gk[:pair]
                mid[rows, lanes] = gv[:pair]
                put_blocks(acc0, block, gk[pair:].astype(F32), 2 * g)
                put_blocks(acc1, block, gv[pair:].astype(F32), 2 * g)
                nft[rows, lanes] = take_heads(gq, first).astype(BF)
            if g == 0:
                xhat, _ = normalise(cs[rows_t].astype(F32))
                nl = (xhat * gain_a + bias_a).astype(BF)
                attt[pl.ds(pl.multiple_of(i * D, D), D)] = nl.T
            steps_at(i, "seven", g)

        put_flat(gr, base, dot(beside(attt, T // TA, D), nft[:, lanes]).astype(BF))
        steps("sevenend", g)

        keys, values = (acc0, kts, cott, 1), (acc1, vts, mid, 2)
        for turn, both in enumerate(((keys, values),) if g == 0 else ((values,), (keys,))):
            count = 8 // len(both)

            @pl.loop(0, BLK // count)
            def _(it):
                low, high = halves[0], halves[1]
                jobs, outs = [], []
                for u in range(count):
                    t = it * count + u
                    every = pl.ds(t, NB, stride=GAP)
                    trow = pl.ds(pl.multiple_of(t * NB, NB), NB)
                    for acc, near, _, _ in both:
                        x = jnp.concatenate([acc[2 * g, every], acc[2 * g + 1, every]], axis=1)
                        jobs.append((acc, every, x.astype(BF), near[trow, lanes]))
                spread = [spread_even(x, low, high) for _, _, x, _ in jobs]
                nears = [spread_pair(n) for _, _, _, n in jobs]
                gm[g] += dot_nt(
                    jnp.concatenate(spread, axis=1), jnp.concatenate(nears, axis=1)
                )
                for (acc, every, _, _), x in zip(jobs, spread):
                    outs.append((acc, every, dot(mcatt[g], x)))
                for acc, every, back in outs:
                    acc[2 * g, every] = back[:NB, :128]
                    acc[2 * g + 1, every] = back[NB:, 128:]
                steps_at(it, "eight", g + turn)

            @pl.loop(0, T // TA)
            def _(i):
                rows = pl.ds(pl.multiple_of(i * TA, TA), TA)
                for acc, _, part, _ in both:
                    far = get_blocks(acc, i * (TA // BLK), TA // BLK, (2 * g, 2 * g + 1))
                    part[rows, lanes] = (part[rows, lanes].astype(F32) + far).astype(BF)

            nlt = beside(attt, T // TA, D)
            for _, _, part, n in both:
                put_flat(gr, base + n * 1024, dot(nlt, part[:, lanes]).astype(BF))
            steps("nine", g + turn)

    grads = []
    for g in range(2):
        tiles = []
        for p in range(2):
            lanes = slice(p * NB, (p + 1) * NB)
            tiles.append(jnp.concatenate([gm[g, :NB, lanes], gm[g, NB:, lanes]], axis=1))
        grad = jnp.concatenate(tiles, axis=0) * psave[2 * SINK - 1, g]
        grads.append(jnp.where(before, grad, 0.0))

    def sweep_back(n, grads):
        it = SINK - 1 - n
        for m in (1, 0):
            grads = [settle_back(x, psave[2 * it + m, g]).T for g, x in enumerate(grads)]
        return tuple(grads)

    grads = lax.fori_loop(0, SINK, sweep_back, tuple(grads))
    grads = [jnp.where(allowed, x, 0.0) for x in grads]
    grad = jnp.concatenate([x[c : c + NB] for x in grads for c in (0, NB)], axis=1)
    glog = jnp.zeros((NB, HEADS * SPAN), F32)
    for s in range(3):
        mine_rows = (row >= firsts[s]) & (row < lasts[s])
        kept = jnp.where(mine_rows, grad, 0.0).astype(BF)
        glog = glog + dot_nt(kept, (gap == firsts[s]).astype(BF))
    glog = glog.astype(BF)
    if gz.shape[0] > 1024:
        gz[...] = jnp.zeros_like(gz)
    put_flat(gz, 0, dot(summ[...].astype(BF).T, glog).astype(BF))
    steps("ten")
    summ[...] = dot_nt(glog, wsort[...]) * (1.0 / BLK)

    @pl.loop(0, T // TA)
    def _(i):
        rows = pl.ds(pl.multiple_of(i * TA, TA), TA)
        gp = jnp.concatenate([nft[rows], cott[rows], mid[rows]], axis=1)
        nb = TA // BLK
        gs = summ[pl.ds(pl.multiple_of(i * nb, nb), nb)]
        gn = dot_nt(gp, wqkv[...]) + jnp.broadcast_to(
            gs[:, None, :], (nb, BLK, D)
        ).reshape(TA, D)
        xhat, rstd = normalise(cs[rows].astype(F32))
        vb[8:9] += jnp.sum(gn * xhat, axis=0, keepdims=True)
        vb[9:10] += jnp.sum(gn, axis=0, keepdims=True)
        gx = nf[rows].astype(F32) + normalise_back(gn, xhat, rstd, gain_a)
        actb[rows] = gx.astype(BF)
        put_end(i, 1, actb)
        steps_at(i, "eleven")

    steps("tail")
    vec_o[...] = vb[...]
    wait_end(0, gpreb)
    wait_end(1, actb)
    there = ends_o.at[pl.ds(pl.multiple_of((1 - sec) * T, T), T)]
    remote(there, there, end_send.at[0], end_recv.at[0], flat.peer(0, 1)).wait_recv()
    for part in packets:
        part.sent(gr)


VM = pl.BlockSpec(memory_space=pltpu.VMEM)
HB = pl.BlockSpec(memory_space=pl.ANY)
SM = pl.BlockSpec(memory_space=pltpu.SMEM)


def layer(dp, tokens, cotangent, lengths, w_qkv, w_out, w_sort, vectors, w_up, b_up, w_down):
    sds = jax.ShapeDtypeStruct
    big = pltpu.VMEM((T, D), BF)
    copies = copies_of(dp)
    return pl.pallas_call(
        functools.partial(kernel, dp),
        out_shape=(
            sds((2 * T, D), BF),
            sds((6 * 4096, 128), BF),
            sds((max(1024, 32 * dp), 128), BF),
            sds((16, D), F32),
        ),
        in_specs=[SM, HB, HB, HB] + [VM] * 7 + [HB, VM, HB],
        out_specs=(HB, HB, HB, VM),
        scratch_shapes=[
            pltpu.VMEM((8192, 128), BF),
            pltpu.VMEM((D, 3 * D), BF),
            pltpu.VMEM((8192, 128), BF),
            pltpu.VMEM((8192, 128), BF),
            big,
            big,
            big,
            big,
            big,
            big,
            big,
            big,
            big,
            pltpu.VMEM((2 * T, TA), BF),
            big,
            big,
            big,
            big,
            pltpu.VMEM((D // 128, NB * GAP, 128), F32),
            pltpu.VMEM((D // 128, NB * GAP, 128), F32),
            pltpu.VMEM((2, 2 * NB, 2 * NB), BF),
            pltpu.VMEM((2, 2 * NB, 2 * NB), BF),
            pltpu.VMEM((2 * SINK, 2, 2 * NB, 2 * NB), F32),
            pltpu.VMEM((NB, D), F32),
            pltpu.VMEM((2, 2 * NB, 2 * NB), F32),
            pltpu.VMEM((2, NB, 128), BF),
            big,
            big,
            pltpu.VMEM((6 * 4096, 128), BF),
            pltpu.VMEM((max(1024, 32 * dp), 128), BF),
            pltpu.VMEM((16, D), F32),
            pltpu.VMEM((copies, 16, D), F32),
            pltpu.SemaphoreType.DMA((5,)),
            pltpu.SemaphoreType.DMA((12,)),
            pltpu.SemaphoreType.DMA((12, 8)),
            pltpu.SemaphoreType.DMA((10,)),
            pltpu.SemaphoreType.DMA((2,)),
            pltpu.SemaphoreType.DMA((1,)),
        ],
        compiler_params=pltpu.CompilerParams(
            vmem_limit_bytes=64 * 1024 * 1024, collective_id=0, has_side_effects=True
        ),
    )(lengths, tokens, cotangent, w_qkv, w_out, w_sort, *vectors, w_up, b_up, w_down)


def widen_kernel(
    ends_i, grads_i, sort_i, vec_i, ends_o, gup_o, gdown_o, gqkv_o, gout_o, gsort_o, v0_o, v1_o, v2_o, v3_o, v4_o, bup_o,
    ein, gin, zin, est, gst, esem, gsem, zsem, eout, gout,
):
    rows_e = 256
    steps = 2 * T // rows_e

    def e_in(i):
        rows = pl.ds(pl.multiple_of(i * rows_e, rows_e), rows_e)
        return pltpu.make_async_copy(ends_i.at[rows], ein.at[rows], esem.at[i])

    def g_in(p):
        rows = pl.ds(pl.multiple_of(p * 4096, 4096), 4096)
        return pltpu.make_async_copy(grads_i.at[rows], gin.at[rows], gsem.at[p])

    def e_out(i, count=rows_e, skip=0):
        rows = pl.ds(pl.multiple_of(i * rows_e + skip, count), count)
        slot = lax.rem(i, 8)
        part = est.at[slot, pl.ds(skip, count)]
        return pltpu.make_async_copy(part, ends_o.at[0, rows], eout.at[slot])

    jobs = []
    for p in range(4):
        part = pl.ds(p * FC, FC)
        jobs.append((p, gin, p * 4096, 4, gup_o.at[:, part]))
        jobs.append((p, gin, p * 4096 + 2048, 4, gdown_o.at[part]))
    jobs.append((4, gin, GOUT, 4, gout_o))
    for g, base in enumerate((GQ0, GQ1)):
        for n in range(3):
            jobs.append((5, gin, base + n * 1024, 2, gqkv_o.at[:, pl.ds(n * D + g * GL, GL)]))
    jobs.append((6, zin, 0, 2, gsort_o))

    def job_out(n, count=D, skip=0):
        _, _, _, tiles, to = jobs[n]
        rows = pl.ds(skip, count)
        part = gst.at[n % 5, rows, pl.ds(0, tiles * 128)]
        return pltpu.make_async_copy(part, to.at[rows], gout.at[n % 5])

    for i in range(steps):
        e_in(i).start()
    for p in range(6):
        g_in(p).start()
    z_in = pltpu.make_async_copy(sort_i.at[pl.ds(0, 1024)], zin, zsem.at[0])
    z_in.start()
    for n, vec_o in zip((8, 9, 0, 1, 2), (v0_o, v1_o, v2_o, v3_o, v4_o)):
        vec_o[...] = vec_i[n : n + 1]
    for n in range(4):
        bup_o[:, n * D : (n + 1) * D] = vec_i[4 + n : 5 + n]

    @pl.loop(0, steps)
    def _(i):
        @pl.when(i >= 8)
        def _():
            e_out(i - 8).wait()

        e_in(i).wait()
        rows = pl.ds(pl.multiple_of(i * rows_e, rows_e), rows_e)
        est[lax.rem(i, 8)] = ein[rows].astype(F32)
        for n in range(2):
            e_out(i, rows_e // 2, n * (rows_e // 2)).start()

    z_in.wait()
    for n, (p, source, base, tiles, _) in enumerate(jobs):
        if p < 5 and (n == 0 or jobs[n - 1][0] != p):
            g_in(p).wait()
        if n == 8:
            g_in(5).wait()
        if n >= 5:
            job_out(n - 5).wait()
        for c in range(tiles):
            gst[n % 5, :, c * 128 : (c + 1) * 128] = source[
                base + c * 512 : base + (c + 1) * 512
            ].astype(F32)
        for m in range(4):
            job_out(n, D // 4, m * (D // 4)).start()
    for n in range(len(jobs) - 5, len(jobs)):
        job_out(n).wait()
    for i in range(steps - 8, steps):
        e_out(i).wait()


def widen(ends, grads, sort, vec):
    sds = jax.ShapeDtypeStruct
    return pl.pallas_call(
        widen_kernel,
        out_shape=(
            sds((1, 2 * T, D), F32),
            sds((D, FF), F32),
            sds((FF, D), F32),
            sds((D, 3 * D), F32),
            sds((D, D), F32),
            sds((D, HEADS * SPAN), F32),
        )
        + (sds((1, D), F32),) * 5
        + (sds((1, FF), F32),),
        in_specs=[HB] * 3 + [VM],
        out_specs=(HB,) * 6 + (VM,) * 6,
        scratch_shapes=[
            pltpu.VMEM((2 * T, D), BF),
            pltpu.VMEM((6 * 4096, 128), BF),
            pltpu.VMEM((1024, 128), BF),
            pltpu.VMEM((8, 256, D), F32),
            pltpu.VMEM((5, D, D), F32),
            pltpu.SemaphoreType.DMA((16,)),
            pltpu.SemaphoreType.DMA((6,)),
            pltpu.SemaphoreType.DMA((1,)),
            pltpu.SemaphoreType.DMA((8,)),
            pltpu.SemaphoreType.DMA((5,)),
        ],
        compiler_params=pltpu.CompilerParams(vmem_limit_bytes=62 * 1024 * 1024),
    )(ends, grads, sort, vec)


def shards(
    dp,
    tokens,
    lengths,
    w_qkv,
    w_out,
    w_sort,
    gain_attn,
    bias_attn,
    gain_ffn,
    bias_ffn,
    w_up,
    bias_up,
    w_down,
    bias_down,
    cotangent,
):
    vectors = [v[None] for v in (gain_attn, bias_attn, gain_ffn, bias_ffn, bias_down)]
    results = layer(
        dp,
        tokens,
        cotangent,
        lengths,
        w_qkv,
        w_out,
        w_sort,
        vectors,
        w_up,
        bias_up[None],
        w_down,
    )
    ends, gup, gdown, gqkv, gout, gsort, *small = widen(*results)
    g_attn, b_attn, g_ffn, b_ffn, b_down, b_up = (v.reshape(-1) for v in small)
    return (
        ends,
        gqkv,
        gout,
        gsort,
        g_attn,
        b_attn,
        g_ffn,
        b_ffn,
        gup,
        b_up,
        gdown,
        b_down,
    )


def solution(mesh):
    rep = [P()] * 11
    return jax.shard_map(
        functools.partial(shards, mesh.shape["dp"]),
        mesh=mesh,
        in_specs=(P("dp", None), P("dp", None), *rep, P("dp", None)),
        out_specs=(P("section", "dp", None), *rep),
        check_vma=False,
    )
```

```python
import functools
import math

import jax
import jax.numpy as jnp
from jax import lax
from jax.experimental import pallas as pl
from jax.experimental.pallas import tpu as pltpu
from jax.sharding import PartitionSpec as P

D = 512
HEADS = 8
HDIM = 64
FF = 2048
BLK = 32
SINK = 8
SPAN = 32
T = 2048
NB = T // BLK
TA = 256
TF = 512
FC = 512
GL = 256
GOUT, GQ0, GQ1 = 16384, 18432, 21504
ORDER = ((0, 1, 2), (1, 0, 2))
PIECE = 512
GAP = BLK + 1
SCALE = 1.0 / math.sqrt(HDIM)
BF = jnp.bfloat16
F32 = jnp.float32


def dot(a, b):
    return jnp.dot(a, b, preferred_element_type=F32)


def dot_nt(a, b):
    return lax.dot_general(a, b, (((1,), (1,)), ((), ())), preferred_element_type=F32)


def iota(shape, axis):
    return lax.broadcasted_iota(jnp.int32, shape, axis)


def normalise(x):
    xc = x - jnp.mean(x, axis=-1, keepdims=True)
    rstd = lax.rsqrt(jnp.mean(xc * xc, axis=-1, keepdims=True) + 1e-5)
    return xc * rstd, rstd


def normalise_back(g, xhat, rstd, gain):
    gg = g * gain
    return rstd * (
        gg
        - jnp.mean(gg, axis=-1, keepdims=True)
        - xhat * jnp.mean(gg * xhat, axis=-1, keepdims=True)
    )


def spread_heads(x, low, high):
    a, b = x[:, :128], x[:, 128:]
    z = jnp.zeros_like(a)
    rows = ([a * low, z], [a * high, z], [z, b * low], [z, b * high])
    return jnp.concatenate([jnp.concatenate(r, axis=1) for r in rows], axis=0)


def take_heads(x, first):
    r = x.shape[0] // 4
    tiles = [
        jnp.where(first, x[2 * c * r : (2 * c + 1) * r, c * 128 : (c + 1) * 128],
                  x[(2 * c + 1) * r : (2 * c + 2) * r, c * 128 : (c + 1) * 128])
        for c in range(2)
    ]
    return jnp.concatenate(tiles, axis=1)


def spread_even(x, low, high):
    a, b = x[:, :128], x[:, 128:]
    rows = ([a * low, b * low], [a * high, b * high])
    return jnp.concatenate([jnp.concatenate(r, axis=1) for r in rows], axis=0)


def spread_pair(x):
    z = jnp.zeros_like(x[:, :128])
    rows = ([x[:, :128], z], [z, x[:, 128:]])
    return jnp.concatenate([jnp.concatenate(r, axis=1) for r in rows], axis=0)


def beside(ref, count, rows):
    return jnp.concatenate([ref[n * rows : (n + 1) * rows] for n in range(count)], axis=1)


def settle(x):
    y = x.reshape(2, NB, 2 * NB)
    y = y - jnp.max(y, axis=1, keepdims=True)
    ex = jnp.exp(y)
    tot = jnp.sum(ex, axis=1, keepdims=True)
    return (ex * inverse(tot)).reshape(x.shape), (y - jnp.log(tot)).reshape(x.shape)


def settle_back(g, p):
    tot = jnp.sum(g.reshape(2, NB, 2 * NB), axis=1, keepdims=True)
    return g - (p.reshape(2, NB, 2 * NB) * tot).reshape(g.shape)


def wide(acc, rows, lanes=range(D // 128)):
    return jnp.concatenate([acc[c, rows] for c in lanes], axis=1)


def put_wide(acc, rows, value):
    for c in range(value.shape[1] // 128):
        acc[c, rows] = value[:, c * 128 : (c + 1) * 128]


def add_wide(acc, rows, value):
    for c in range(value.shape[1] // 128):
        acc[c, rows] += value[:, c * 128 : (c + 1) * 128]


def block_rows(block):
    return pl.ds(block * GAP, BLK)


def get_blocks(acc, first, count, lanes=range(D // 128)):
    return jnp.concatenate([wide(acc, block_rows(first + n), lanes) for n in range(count)], axis=0)


def put_blocks(acc, first, value, lane=0):
    for n in range(value.shape[0] // BLK):
        for c in range(value.shape[1] // 128):
            part = value[n * BLK : (n + 1) * BLK, c * 128 : (c + 1) * 128]
            acc[lane + c, block_rows(first + n)] = part


def flat_rows(ref, base, step, count):
    parts = [ref[pl.ds(pl.multiple_of(base + c * step, 16), count)] for c in range(D // 128)]
    return jnp.concatenate(parts, axis=1)


def put_flat(ref, base, value):
    rows = value.shape[0]
    for c in range(value.shape[1] // 128):
        ref[pl.ds(pl.multiple_of(base + c * rows, 16), rows)] = value[:, c * 128 : (c + 1) * 128]


def inverse(x):
    r = pl.reciprocal(x, approx=True)
    return r * (2.0 - x * r)


def gelu_both(u):
    c = math.sqrt(2.0 / math.pi)
    e = -2.0 * c / math.log(2.0)
    u2 = u * u
    power = jnp.minimum(u * (e + (e * 0.044715) * u2), 120.0)
    half = pl.reciprocal(1.0 + jnp.exp2(power), approx=True)
    act = u * half
    slope = half + act * (1.0 - half) * (2.0 * c + (6.0 * c * 0.044715) * u2)
    return act, slope


AXES = {16: ((1, 2), (2, 2), (4, 4)), 128: ((1, 4), (32, 4), (4, 8))}


def axes_of(dp):
    if dp in AXES:
        return AXES[dp]
    a = max(n for n in range(1, dp + 1) if dp % (n * n) == 0)
    return (1, a), (a, a), (a * a, dp // (a * a))


class Links:
    def __init__(self, groups):
        self.sec, self.dp = lax.axis_index("section"), lax.axis_index("dp")
        self.levels = []
        for axes in groups:
            own = [lax.rem(lax.div(self.dp, stride), n) for stride, n in axes]
            me, scale = 0, 1
            for (_, n), at in zip(axes, own):
                me, scale = me + at * scale, scale * n
            self.levels.append((axes, own, me))
        self.sizes = [2] + [math.prod(n for _, n in axes) for axes in groups]
        self.first = [0]
        for n in self.sizes:
            self.first.append(self.first[-1] + n - 1)
        self.copies = self.first[-1]

    def place(self, level, k):
        return lax.rem(self.levels[level - 1][2] + k, self.sizes[level])

    def peer(self, level, k):
        if level == 0:
            return (1 - self.sec, self.dp)
        axes, own, _ = self.levels[level - 1]
        place, to = self.place(level, k), self.dp
        for (stride, n), at in zip(axes, own):
            to = to + (lax.rem(place, n) - at) * stride
            place = lax.div(place, n)
        return (self.sec, to)

    def everyone(self):
        return [
            self.peer(level, k)
            for level in range(len(self.sizes))
            for k in range(1, self.sizes[level])
        ]


def all_links(dp):
    a, b, c = axes_of(dp)
    sec = lax.axis_index("section")
    a1 = (a[0] + sec * (b[0] - a[0]), a[1])
    b1 = (b[0] + sec * (a[0] - b[0]), b[1])
    return Links([[a1], [b1], [c]]), Links([[a, b], [c]])


def copies_of(dp):
    a, b, c = axes_of(dp)
    return a[1] * b[1] + c[1] - 1


def remote(src, dst, ssem, rsem, device):
    return pltpu.make_async_remote_copy(
        src_ref=src,
        dst_ref=dst,
        send_sem=ssem,
        recv_sem=rsem,
        device_id=device,
        device_id_type=pl.DeviceIdType.MESH,
    )


class Packet:
    def __init__(self, links, ref, out, base, rows, inboxes, ssem, rsem, osem, number):
        self.links, self.ref, self.out, self.inboxes = links, ref, out, inboxes
        self.ssem, self.rsem, self.osem, self.number = ssem, rsem, osem, number
        self.deep = len(links.sizes)
        self.last = 2 * self.deep
        half = rows // 2
        self.size = [half]
        self.off = [base + links.sec * half]
        self.away = base + (1 - links.sec) * half
        self.inpos = [0, 0 if inboxes[0] is not inboxes[1] else half]
        for level in range(1, self.deep):
            n = links.sizes[level]
            self.size.append(self.size[-1] // n)
            self.off.append(self.off[-1] + links.place(level, 0) * self.size[-1])
            self.inpos.append(self.inpos[-1] + (n - 1) * self.size[-1])

    def rows(self, ref, off, level):
        return ref.at[pl.ds(pl.multiple_of(off, 16), self.size[level])]

    def landing(self, level, k, skip, count):
        box, base = self.inboxes[min(level, 1)]
        at = base + self.inpos[level] + (k - 1) * self.size[level] + skip
        return box, pl.ds(pl.multiple_of(at, 16), count)

    def pieces(self, level):
        count = -(-self.size[level] // PIECE)
        rows = self.size[level] // count
        return [(n * rows, rows) for n in range(count)]

    def reduce_start(self, level, k):
        off = self.away
        if level > 0:
            off = self.off[level - 1] + self.links.place(level, k) * self.size[level]
        for skip, count in self.pieces(level):
            box, rows = self.landing(level, k, skip, count)
            remote(
                self.ref.at[pl.ds(pl.multiple_of(off + skip, 16), count)],
                box.at[rows],
                self.ssem.at[self.number],
                self.rsem.at[self.number, level],
                self.links.peer(level, k),
            ).start()

    def gather_start(self, level, k):
        source = self.ref if level == self.deep - 1 else self.out
        for skip, count in self.pieces(level):
            rows = pl.ds(pl.multiple_of(self.off[level] + skip, 16), count)
            remote(
                source.at[rows],
                self.out.at[rows],
                self.ssem.at[self.number],
                self.rsem.at[self.number, self.deep + level],
                self.links.peer(level, k),
            ).start()

    def arrived(self, level, gathered):
        count = (self.links.sizes[level] - 1) * self.size[level]
        if count == 0:
            return
        if not gathered:
            box, rows = self.landing(level, 1, 0, count)
            what = box.at[rows]
        else:
            base = self.away if level == 0 else self.off[level - 1]
            what = self.out.at[pl.ds(pl.multiple_of(base, 16), count)]
        sem = self.rsem.at[self.number, level + (self.deep if gathered else 0)]
        remote(what, what, self.ssem.at[self.number], sem, self.links.peer(0, 1)).wait_recv()

    def sent(self, source):
        count = 2 * sum((n - 1) * size for n, size in zip(self.links.sizes, self.size))
        what = source.at[pl.ds(0, count)]
        sem = self.rsem.at[self.number, 0]
        remote(what, what, self.ssem.at[self.number], sem, self.links.peer(0, 1)).wait_send()

    def own_copy(self):
        return pltpu.make_async_copy(
            self.rows(self.ref, self.off[-1], -1),
            self.rows(self.out, self.off[-1], -1),
            self.osem.at[self.number],
        )

    def ks(self, level):
        return range(1, self.links.sizes[level])

    def add(self, level):
        size = self.size[level]
        chunk = size // -(-size // 1024)
        wide_sum = self.links.sizes[level] > 2

        @pl.loop(0, size // chunk)
        def _(j):
            rows = pl.ds(pl.multiple_of(self.off[level] + j * chunk, 16), chunk)
            total = self.ref[rows]
            if wide_sum:
                total = total.astype(F32)
            for k in self.ks(level):
                box, came = self.landing(level, k, j * chunk, chunk)
                total += box[came].astype(total.dtype)
            self.ref[rows] = total.astype(BF)

    def step(self, n):
        deep = self.deep
        if 1 <= n <= deep:
            self.arrived(n - 1, False)
            self.add(n - 1)
        if n == deep:
            self.own_copy().start()
        if n == deep + 1:
            self.own_copy().wait()
        if n > deep:
            self.arrived(self.last - n, True)
        if n < deep:
            for k in self.ks(n):
                self.reduce_start(n, k)
        elif n < self.last:
            for k in self.ks(self.last - 1 - n):
                self.gather_start(self.last - 1 - n, k)


PLAN = {
    ("ffnend", 0): (("f0", 0),),
    ("ffn", 1, 1): (("f0", 1),),
    ("ffnend", 1): (("f1", 0),),
    ("ffn", 2, 0): (("f0", 2),),
    ("ffn", 2, 1): (("f1", 1),),
    ("ffn", 2, 3): (("f0", 3),),
    ("ffnend", 2): (("f2", 0),),
    ("ffn", 3, 0): (("f1", 2),),
    ("ffn", 3, 1): (("f2", 1),),
    ("ffn", 3, 3): (("f0", 4), ("f1", 3),),
    ("ffnend", 3): (("f3", 0),),
    ("six", 0): (("f2", 2),),
    ("six", 3): (("f3", 1),),
    ("six", 7): (("f0", 5),),
    ("sixend",): (("o", 0),),
    ("seven", 0, 2): (("f3", 2),),
    ("seven", 0, 3): (("f1", 4), ("o", 1),),
    ("seven", 0, 4): (("f2", 3), ("f0", 6),),
    ("seven", 0, 6): (("f3", 3),),
    ("eight", 0, 0): (("o", 2),),
    ("nine", 0): (("f1", 5), ("f0", 7), ("q0", 0),),
    ("seven", 1, 1): (("f2", 4),),
    ("seven", 1, 2): (("o", 3),),
    ("seven", 1, 3): (("f0", 8), ("f1", 6),),
    ("seven", 1, 4): (("q0", 1), ("f3", 4),),
    ("nine", 1): (("f2", 5), ("f1", 7), ("qv", 0),),
    ("eight", 2, 0): (("o", 4),),
    ("eight", 2, 2): (("q0", 2),),
    ("nine", 2): (("f1", 8), ("qv", 1), ("qk", 0),),
    ("ten",): (("f2", 6), ("f3", 5), ("q0", 3), ("qk", 1), ("o", 5), ("z2", 0),),
    ("eleven", 1): (("qv", 2),),
    ("eleven", 2): (("z2", 1),),
    ("eleven", 4): (("f2", 7),),
    ("eleven", 5): (("q0", 4), ("f3", 6),),
    ("eleven", 6): (("qv", 3),),
    ("eleven", 7): (("f2", 8), ("qk", 2), ("o", 6),),
    ("tail",): (
        ("va", 0), ("z2", 2), ("va", 1), ("q0", 5), ("f3", 7), ("qv", 4), ("qk", 3), ("o", 7),
        ("z2", 3), ("va", 2), ("f3", 8), ("q0", 6), ("o", 8), ("qk", 4), ("va", 3), ("z2", 4),
        ("qv", 5), ("q0", 7), ("qv", 6), ("qk", 5), ("q0", 8), ("z2", 5), ("qk", 6), ("z2", 6),
    ),
}


def kernel(
    dp,
    len_ref,
    tok_ref,
    cot_ref,
    wqkv_ref,
    wout,
    wsort,
    gain_a_ref,
    bias_a_ref,
    gain_f_ref,
    bias_f_ref,
    bias_d_ref,
    wup,
    bup,
    wdown,
    ends_o,
    grads_o,
    sort_o,
    vec_o,
    xs,
    wqkv,
    w1,
    w2,
    cs,
    qs,
    ks,
    vs,
    kts,
    vts,
    kfs,
    vfs,
    ps,
    attt,
    mid,
    nf,
    nft,
    cott,
    acc0,
    acc1,
    mcat,
    mcatt,
    psave,
    summ,
    gm,
    halves,
    actb,
    gpreb,
    gr,
    gz,
    vb,
    vin,
    sem_in,
    ssem,
    rsem,
    out_sem,
    end_send,
    end_recv,
):
    deep, flat = all_links(dp)
    sec = deep.sec
    mine = pl.ds(pl.multiple_of(sec * T, T), T)
    for c in range(4):
        lanes = slice(c * 128, (c + 1) * 128)
        pltpu.make_async_copy(
            tok_ref.at[mine, lanes], xs.at[pl.ds(c * T, T)], sem_in.at[0]
        ).start()
    e0 = len_ref[sec, 0]
    e1 = e0 + len_ref[sec, 1]
    gain_a, bias_a = gain_a_ref[...], bias_a_ref[...]
    gain_f, bias_f = gain_f_ref[...], bias_f_ref[...]
    bias_d = bias_d_ref[...]
    vb[...] = jnp.zeros_like(vb)
    w_copy = pltpu.make_async_copy(wqkv_ref, wqkv, sem_in.at[4])
    w_copy.start()
    x_part = xs.at[pl.ds(0, 4 * T)]
    pltpu.make_async_copy(x_part, x_part, sem_in.at[0]).wait()
    w_copy.wait()
    cot_copy = pltpu.make_async_copy(cot_ref.at[mine], cs, sem_in.at[1])
    cot_copy.start()
    for c in range(FF // FC):
        for l in range(4):
            to = pl.ds((c * 4 + l) * FC, FC)
            lane = l * 128
            pltpu.make_async_copy(
                wup.at[:, pl.ds(c * FC + lane, 128)], w1.at[to], sem_in.at[2]
            ).start()
            pltpu.make_async_copy(
                wdown.at[pl.ds(c * FC, FC), pl.ds(lane, 128)], w2.at[to], sem_in.at[3]
            ).start()

    def packet(number, base, rows, links, box, more=None, ref=gr, out=grads_o):
        boxes = (box, box if more is None else more)
        return Packet(links, ref, out, base, rows, boxes, ssem, rsem, out_sem, number)

    boxes = ((xs, 0), (xs, 4096), (w1, 0), (w2, 0))
    f = [packet(p, p * 4096, 4096, deep, boxes[p]) for p in range(4)]
    parts = dict(f0=f[0], f1=f[1], f2=f[2], f3=f[3])
    if 1024 % (32 * dp) == 0:
        parts["o"] = packet(4, GOUT, 2048, deep, (w1, 4096))
        parts["q0"] = packet(5, GQ0, 3072, deep, (w2, 4096))
        parts["qk"] = packet(6, GQ1, 1024, flat, (w1, 0))
        parts["qv"] = packet(7, GQ1 + 1024, 2048, flat, (w1, 6144))
        parts["z2"] = packet(9, 0, 1024, flat, (w2, 7168), ref=gz, out=sort_o)
    else:
        parts["qk"] = packet(4, GOUT, 8192, flat, (w1, 0))
        parts["z2"] = packet(5, 0, gz.shape[0], flat, (w2, 4096), ref=gz, out=sort_o)

    class Vectors:
        def __init__(self, number, base, count):
            self.number, self.rows = number, pl.ds(base, count)

        def copy(self, level, k):
            at = flat.first[level] + k - 1
            return remote(
                vb.at[self.rows],
                vin.at[at, self.rows],
                ssem.at[self.number],
                rsem.at[self.number, level],
                flat.peer(level, k),
            )

        def step(self, n):
            if n >= 1:
                first, count = flat.first[n - 1], flat.sizes[n - 1] - 1
                if count:
                    came = vin.at[pl.ds(first, count), self.rows]
                    sem = rsem.at[self.number, n - 1]
                    both = remote(came, came, ssem.at[self.number], sem, flat.peer(0, 1))
                    both.wait_send()
                    both.wait_recv()
                for k in range(count):
                    vb[self.rows] += vin[first + k, self.rows]
            if n < len(flat.sizes):
                for k in range(1, flat.sizes[n]):
                    self.copy(n, k).start()

    packets = list(parts.values())
    parts["va"] = Vectors(10, 0, 16)
    def steps(*where):
        for name, n in PLAN.get(where, ()):
            if name in parts:
                parts[name].step(n)

    def steps_at(i, *where):
        for place in PLAN:
            if place[:-1] == where:

                @pl.when(i == place[-1])
                def _():
                    steps(*place)

    def end_copies(at, count, far_sec, staged):
        tile = staged.at[pl.ds(pl.multiple_of(at, TA), count)]
        there = ends_o.at[pl.ds(pl.multiple_of(sec * T + at, TA), count)]
        away = remote(tile, there, end_send.at[far_sec], end_recv.at[0], flat.peer(0, 1))
        return away, pltpu.make_async_copy(tile, there, end_send.at[far_sec])

    def put_end(i, far_sec, staged):
        away, here = end_copies(i * TA, TA, far_sec, staged)

        @pl.when(sec == far_sec)
        def _():
            away.start()

        @pl.when(sec != far_sec)
        def _():
            here.start()

    def wait_end(far_sec, staged):
        away, here = end_copies(0, T, far_sec, staged)

        @pl.when(sec == far_sec)
        def _():
            away.wait_send()

        @pl.when(sec != far_sec)
        def _():
            here.wait()

    lane = iota((NB, 128), 1)
    halves[0] = (lane < HDIM).astype(BF)
    halves[1] = (lane >= HDIM).astype(BF)

    @pl.loop(0, T // TA)
    def _(i):
        rows = pl.ds(pl.multiple_of(i * TA, TA), TA)
        xhat, _ = normalise(flat_rows(xs, i * TA, T, TA).astype(F32))
        normed = xhat * gain_a + bias_a
        low = normed.astype(BF)
        packed = dot(low, wqkv[...]).astype(BF)
        qs[rows] = packed[:, :D]
        k, v = packed[:, D : 2 * D], packed[:, 2 * D :]
        ks[rows] = k
        vs[rows] = v
        nb = TA // BLK
        put_blocks(acc0, i * nb, k.astype(F32))
        put_blocks(acc1, i * nb, v.astype(F32))
        summ[pl.ds(pl.multiple_of(i * nb, nb), nb)] = jnp.mean(
            normed.reshape(nb, BLK, D), axis=1
        )

    blk = iota((2 * NB, 2 * NB), 0) & (NB - 1)
    col = iota((2 * NB, 2 * NB), 1) & (NB - 1)
    owner = (blk >= e0).astype(jnp.int32) + (blk >= e1).astype(jnp.int32)
    col_owner = (col >= e0).astype(jnp.int32) + (col >= e1).astype(jnp.int32)
    same = owner == col_owner
    allowed = same & (col <= blk)
    before = same & (col < blk)
    a = iota((HEADS * SPAN, D), 0)
    b = iota((HEADS * SPAN, D), 1)
    gap = jnp.where(a >> 5 == b >> 6, (b & (HDIM - 1)) - (a & (SPAN - 1)), -1000)
    row = iota((NB, D), 0)
    firsts = (jnp.int32(0), e0, e1)
    lasts = (e0, e1, jnp.int32(NB))
    logits = dot(summ[...].astype(BF), wsort[...])
    high = logits.astype(BF)
    rest = logits - high.astype(F32)
    middle = rest.astype(BF)
    three = jnp.concatenate([high, middle, (rest - middle.astype(F32)).astype(BF)], axis=0)
    placed = jnp.zeros((NB, D), F32)
    for s in range(3):
        moved = dot(three, (gap == firsts[s]).astype(BF))
        moved = moved[:NB] + moved[NB : 2 * NB] + moved[2 * NB :]
        placed = jnp.where(row >= firsts[s], moved, placed)
    start = []
    for g in range(2):
        tiles = [placed[:, c : c + 128] for c in (2 * g * 128, (2 * g + 1) * 128)]
        start.append(jnp.where(allowed, jnp.concatenate(tiles, axis=0), -10000.0))

    def sweep(it, cur):
        for n in range(2):
            cur = [x.T for x in cur]
            done = [settle(x) for x in cur]
            for g in range(2):
                psave[2 * it + n, g] = done[g][0]
            cur = [x for _, x in done]
        return tuple(cur)

    lax.fori_loop(0, SINK, sweep, tuple(start))
    for g in range(2):
        mix = jnp.where(before, psave[2 * SINK - 1, g], 0.0)
        mcat[g] = mix.astype(BF)
        for p in range(2):
            tr = mix[p * NB : (p + 1) * NB].T.astype(BF)
            mcatt[g, p * NB : (p + 1) * NB] = jnp.concatenate([tr[:NB], tr[NB:]], axis=1)

    @pl.loop(0, BLK // 4)
    def _(it):
        low, high = halves[0], halves[1]
        jobs, outs = [], []
        for u in range(4):
            t = it * 4 + u
            every = pl.ds(t, NB, stride=GAP)
            for acc, keep in ((acc0, kts), (acc1, vts)):
                x = wide(acc, every).astype(BF)
                keep[pl.ds(pl.multiple_of(t * NB, NB), NB)] = x
                jobs.append((acc, every, x))
        for acc, every, x in jobs:
            for g in range(2):
                far = dot(mcat[g], spread_even(x[:, g * GL : (g + 1) * GL], low, high))
                outs.append((acc, every, g, far))
        for acc, every, g, far in outs:
            acc[2 * g, every] = far[:NB, :128].astype(BF).astype(F32)
            acc[2 * g + 1, every] = far[NB:, 128:].astype(BF).astype(F32)

    pair = 2 * BLK
    srow = iota((2 * pair, GL), 0)
    tcol = iota((2 * pair, GL), 1) & (pair - 1)
    together = (srow & BLK) == (tcol & BLK)
    own_ok = together & (srow < pair) & ((srow & (BLK - 1)) <= (tcol & (BLK - 1)))
    far_ok = together & (srow >= pair)

    cot_copy.wait()

    @pl.loop(0, T // TA)
    def _(i):
        low, high = halves[0], halves[1]
        first = iota((pair, 128), 1) < HDIM
        seen, scores = [], []
        for j in range(TA // pair):
            block = (i * (TA // pair) + j) * 2
            rows = pl.ds(pl.multiple_of(block * BLK, pair), pair)
            kf = get_blocks(acc0, block, 2).astype(BF)
            vf16 = get_blocks(acc1, block, 2).astype(BF)
            kfs[rows] = kf
            vfs[rows] = vf16
            kseen = jnp.concatenate([ks[rows], kf], axis=0)
            seen.append(jnp.concatenate([vs[rows], vf16], axis=0))
            q = qs[rows] * SCALE
            closed = []
            for n in (block, block + 1):
                opening = (n == 0) | (n == e0) | (n == e1)
                closed.append(jnp.where(opening, 0, 1))
            open_far = jnp.where(tcol < BLK, closed[0], closed[1]) == 1
            valid = own_ok | (far_ok & open_far)
            for g in range(2):
                lanes = slice(g * GL, (g + 1) * GL)
                sc = dot_nt(kseen[:, lanes], spread_heads(q[:, lanes], low, high))
                scores.append(jnp.where(valid, sc, -1e9))
        sc = jnp.concatenate(scores, axis=1)
        ex = jnp.exp(sc - jnp.max(sc, axis=0, keepdims=True))
        w16 = (ex * inverse(jnp.sum(ex, axis=0, keepdims=True))).astype(BF)
        ws = [w16[:, c : c + GL] for c in range(0, w16.shape[1], GL)]
        turned = [w.T for w in ws]
        for n, w in enumerate(ws):
            prow = pl.ds(pl.multiple_of((i * (TA // pair) + n // 2) * pair, pair), pair)
            kept = [w[c : c + BLK] + w[c + BLK : c + pair] for c in (0, pair)]
            ps[prow, n % 2 * GL : (n % 2 + 1) * GL] = jnp.concatenate(kept, axis=0)
        products = [
            dot(w, seen[n // 2][:, n % 2 * GL : (n % 2 + 1) * GL]) for n, w in enumerate(turned)
        ]
        made = [take_heads(r, first).astype(BF) for r in products]
        rows = pl.ds(pl.multiple_of(i * TA, TA), TA)
        att = jnp.concatenate(
            [jnp.concatenate(made[n : n + 2], axis=1) for n in range(0, len(made), 2)], axis=0
        )
        for n in range(2):
            at = pl.multiple_of(i * D + n * TA, TA)
            attt[pl.ds(at, TA)] = att[:, n * TA : (n + 1) * TA]
        x = flat_rows(xs, i * TA, T, TA).astype(F32)
        middle = (x + dot(att, wout[...])).astype(BF)
        mid[rows] = middle
        xhat, _ = normalise(middle.astype(F32))
        nf[rows] = (xhat * gain_f + bias_f).astype(BF)

    barrier = pltpu.get_barrier_semaphore()
    everyone = flat.everyone()
    for device in everyone:
        pl.semaphore_signal(
            barrier, inc=1, device_id=device, device_id_type=pl.DeviceIdType.MESH
        )

    @pl.loop(0, T // TF)
    def _(i):
        rows = pl.ds(pl.multiple_of(i * TF, TF), TF)
        nft[rows] = nf[rows].T
        cott[rows] = cs[rows].T
        put_wide(acc0, rows, jnp.zeros((TF, D), F32))
        put_wide(acc1, rows, jnp.zeros((TF, D), F32))

    pltpu.make_async_copy(w1, w1, sem_in.at[2]).wait()
    pltpu.make_async_copy(w2, w2, sem_in.at[3]).wait()
    pl.semaphore_wait(barrier, len(everyone))

    @pl.loop(0, FF // FC)
    def _(c):
        cols = pl.ds(pl.multiple_of(c * FC, FC), FC)
        @pl.loop(0, T // TF)
        def _(i):
            rows = pl.ds(pl.multiple_of(i * TF, TF), TF)
            up = flat_rows(w1, c * 4 * FC, FC, FC)
            down = flat_rows(w2, c * 4 * FC, FC, FC)
            pre = dot(nf[rows], up) + bup[0:1, cols]
            act, slope = gelu_both(pre)
            act = act.astype(BF)
            gact = dot_nt(cs[rows], down)
            gpre = slope * gact
            vb[pl.ds(4 + c, 1)] += jnp.sum(gpre, axis=0, keepdims=True)
            gpre = gpre.astype(BF)
            add_wide(acc0, rows, dot(act, down))
            add_wide(acc1, rows, dot_nt(gpre, up))
            actb[rows] = act
            gpreb[rows] = gpre
            for chunk in range(FF // FC):

                @pl.when(c == chunk)
                def _():
                    steps_at(i, "ffn", chunk)

        gu = dot(beside(nft, T // TF, D), gpreb[...])
        put_flat(gr, c * 4096, gu.astype(BF))
        gd = dot(beside(cott, T // TF, D), actb[...])
        put_flat(gr, c * 4096 + 2048, gd.T.astype(BF))

        steps_at(c, "ffnend")


    @pl.loop(0, T // TA)
    def _(i):
        rows = pl.ds(pl.multiple_of(i * TA, TA), TA)
        mf = mid[rows].astype(F32)
        gpreb[rows] = (mf + wide(acc0, rows) + bias_d).astype(BF)
        put_end(i, 0, gpreb)
        cot = cs[rows].astype(F32)
        gn = wide(acc1, rows)
        xhat, rstd = normalise(mf)
        vb[0:1] += jnp.sum(gn * xhat, axis=0, keepdims=True)
        vb[1:2] += jnp.sum(gn, axis=0, keepdims=True)
        vb[2:3] += jnp.sum(cot, axis=0, keepdims=True)
        nf[rows] = (cot + normalise_back(gn, xhat, rstd, gain_f)).astype(BF)
        steps_at(i, "six")

    x_copy = pltpu.make_async_copy(tok_ref.at[mine], cs, sem_in.at[0])
    x_copy.start()
    for n in range(T // TA):
        tile = [attt[n * D + m * TA : n * D + (m + 1) * TA] for m in range(2)]
        attt[n * D : (n + 1) * D] = jnp.concatenate(tile, axis=1).T
    gout = dot(beside(attt, T // TA, D), nf[...]).astype(BF)
    put_flat(gr, GOUT, gout)
    gm[...] = jnp.zeros_like(gm)
    steps("sixend")
    x_copy.wait()

    for g in range(2):
        lanes = slice(g * GL, (g + 1) * GL)
        base = (GQ0, GQ1)[g]

        @pl.loop(0, T // TA)
        def _(i):
            rows_t = pl.ds(pl.multiple_of(i * TA, TA), TA)
            gat = dot_nt(nf[rows_t], wout[lanes]).astype(BF)
            low, high = halves[0], halves[1]
            first = iota((pair, 128), 1) < HDIM
            block0 = (iota((BLK, GL), 1) & BLK == 0).astype(BF)
            block1 = (iota((BLK, GL), 1) & BLK != 0).astype(BF)
            blocks, spread, gws, w16s = [], [], [], []
            for j in range(TA // pair):
                at = pl.multiple_of((i * (TA // pair) + j) * pair, pair)
                rows = pl.ds(at, pair)
                vseen = jnp.concatenate([vs[rows, lanes], vfs[rows, lanes]], axis=0)
                gad = spread_heads(gat[j * pair : (j + 1) * pair], low, high)
                gws.append(dot_nt(vseen, gad))
                kept = ps[rows, lanes]
                own, far = kept[:BLK], kept[BLK:]
                w16s.append(
                    jnp.concatenate(
                        [own * block0, own * block1, far * block0, far * block1], axis=0
                    )
                )
                blocks.append(rows)
                spread.append(gad)
            w16 = jnp.concatenate(w16s, axis=1)
            gw = jnp.concatenate(gws, axis=1)
            w = w16.astype(F32)
            gs = w * (gw - jnp.sum(gw * w, axis=0, keepdims=True))
            gs = (gs * SCALE).astype(BF)
            gss = [gs[:, c : c + GL] for c in range(0, gs.shape[1], GL)]
            turned = [part.T for part in gss]
            gvs = [dot(w, gad).astype(BF) for w, gad in zip(w16s, spread)]
            gks = [
                dot(part, spread_heads(qs[rows, lanes], low, high)).astype(BF)
                for part, rows in zip(gss, blocks)
            ]
            gqs = []
            for part, rows in zip(turned, blocks):
                kseen = jnp.concatenate([ks[rows, lanes], kfs[rows, lanes]], axis=0)
                gqs.append(dot(part, kseen))
            for j, (rows, gk, gv, gq) in enumerate(zip(blocks, gks, gvs, gqs)):
                block = (i * (TA // pair) + j) * 2
                cott[rows, lanes] = gk[:pair]
                mid[rows, lanes] = gv[:pair]
                put_blocks(acc0, block, gk[pair:].astype(F32), 2 * g)
                put_blocks(acc1, block, gv[pair:].astype(F32), 2 * g)
                nft[rows, lanes] = take_heads(gq, first).astype(BF)
            if g == 0:
                xhat, _ = normalise(cs[rows_t].astype(F32))
                nl = (xhat * gain_a + bias_a).astype(BF)
                attt[pl.ds(pl.multiple_of(i * D, D), D)] = nl.T
            steps_at(i, "seven", g)

        gq = dot(beside(attt, T // TA, D), nft[:, lanes]).astype(BF)
        put_flat(gr, base + ORDER[g].index(0) * 1024, gq)
        steps("sevenend", g)

        keys, values = (acc0, kts, cott, 1), (acc1, vts, mid, 2)
        for turn, both in enumerate(((keys, values),) if g == 0 else ((values,), (keys,))):
            count = 8 // len(both)

            @pl.loop(0, BLK // count)
            def _(it):
                low, high = halves[0], halves[1]
                jobs, outs = [], []
                for u in range(count):
                    t = it * count + u
                    every = pl.ds(t, NB, stride=GAP)
                    trow = pl.ds(pl.multiple_of(t * NB, NB), NB)
                    for acc, near, _, _ in both:
                        x = jnp.concatenate([acc[2 * g, every], acc[2 * g + 1, every]], axis=1)
                        jobs.append((acc, every, x.astype(BF), near[trow, lanes]))
                spread = [spread_even(x, low, high) for _, _, x, _ in jobs]
                nears = [spread_pair(n) for _, _, _, n in jobs]
                gm[g] += dot_nt(
                    jnp.concatenate(spread, axis=1), jnp.concatenate(nears, axis=1)
                )
                for (acc, every, _, _), x in zip(jobs, spread):
                    outs.append((acc, every, dot(mcatt[g], x)))
                for acc, every, back in outs:
                    acc[2 * g, every] = back[:NB, :128]
                    acc[2 * g + 1, every] = back[NB:, 128:]
                steps_at(it, "eight", g + turn)

            @pl.loop(0, T // TA)
            def _(i):
                rows = pl.ds(pl.multiple_of(i * TA, TA), TA)
                for acc, _, part, _ in both:
                    far = get_blocks(acc, i * (TA // BLK), TA // BLK, (2 * g, 2 * g + 1))
                    part[rows, lanes] = (part[rows, lanes].astype(F32) + far).astype(BF)

            nlt = beside(attt, T // TA, D)
            for _, _, part, n in both:
                at = base + ORDER[g].index(n) * 1024
                put_flat(gr, at, dot(nlt, part[:, lanes]).astype(BF))
            steps("nine", g + turn)

    grads = []
    for g in range(2):
        tiles = []
        for p in range(2):
            lanes = slice(p * NB, (p + 1) * NB)
            tiles.append(jnp.concatenate([gm[g, :NB, lanes], gm[g, NB:, lanes]], axis=1))
        grad = jnp.concatenate(tiles, axis=0) * psave[2 * SINK - 1, g]
        grads.append(jnp.where(before, grad, 0.0))

    def sweep_back(n, grads):
        it = SINK - 1 - n
        for m in (1, 0):
            grads = [settle_back(x, psave[2 * it + m, g]).T for g, x in enumerate(grads)]
        return tuple(grads)

    grads = lax.fori_loop(0, SINK, sweep_back, tuple(grads))
    grads = [jnp.where(allowed, x, 0.0) for x in grads]
    grad = jnp.concatenate([x[c : c + NB] for x in grads for c in (0, NB)], axis=1)
    glog = jnp.zeros((NB, HEADS * SPAN), F32)
    for s in range(3):
        mine_rows = (row >= firsts[s]) & (row < lasts[s])
        kept = jnp.where(mine_rows, grad, 0.0).astype(BF)
        glog = glog + dot_nt(kept, (gap == firsts[s]).astype(BF))
    glog = glog.astype(BF)
    if gz.shape[0] > 1024:
        gz[...] = jnp.zeros_like(gz)
    put_flat(gz, 0, dot(summ[...].astype(BF).T, glog).astype(BF))
    steps("ten")
    summ[...] = dot_nt(glog, wsort[...]) * (1.0 / BLK)

    @pl.loop(0, T // TA)
    def _(i):
        rows = pl.ds(pl.multiple_of(i * TA, TA), TA)
        gp = jnp.concatenate([nft[rows], cott[rows], mid[rows]], axis=1)
        nb = TA // BLK
        gs = summ[pl.ds(pl.multiple_of(i * nb, nb), nb)]
        gn = dot_nt(gp, wqkv[...]) + jnp.broadcast_to(
            gs[:, None, :], (nb, BLK, D)
        ).reshape(TA, D)
        xhat, rstd = normalise(cs[rows].astype(F32))
        vb[8:9] += jnp.sum(gn * xhat, axis=0, keepdims=True)
        vb[9:10] += jnp.sum(gn, axis=0, keepdims=True)
        gx = nf[rows].astype(F32) + normalise_back(gn, xhat, rstd, gain_a)
        actb[rows] = gx.astype(BF)
        put_end(i, 1, actb)
        steps_at(i, "eleven")

    steps("tail")
    vec_o[...] = vb[...]
    wait_end(0, gpreb)
    wait_end(1, actb)
    there = ends_o.at[pl.ds(pl.multiple_of((1 - sec) * T, T), T)]
    remote(there, there, end_send.at[0], end_recv.at[0], flat.peer(0, 1)).wait_recv()
    for part in packets:
        part.sent(gr)


VM = pl.BlockSpec(memory_space=pltpu.VMEM)
HB = pl.BlockSpec(memory_space=pl.ANY)
SM = pl.BlockSpec(memory_space=pltpu.SMEM)


def layer(dp, tokens, cotangent, lengths, w_qkv, w_out, w_sort, vectors, w_up, b_up, w_down):
    sds = jax.ShapeDtypeStruct
    big = pltpu.VMEM((T, D), BF)
    copies = copies_of(dp)
    return pl.pallas_call(
        functools.partial(kernel, dp),
        out_shape=(
            sds((2 * T, D), BF),
            sds((6 * 4096, 128), BF),
            sds((max(1024, 32 * dp), 128), BF),
            sds((16, D), F32),
        ),
        in_specs=[SM, HB, HB, HB] + [VM] * 7 + [HB, VM, HB],
        out_specs=(HB, HB, HB, VM),
        scratch_shapes=[
            pltpu.VMEM((8192, 128), BF),
            pltpu.VMEM((D, 3 * D), BF),
            pltpu.VMEM((8192, 128), BF),
            pltpu.VMEM((8192, 128), BF),
            big,
            big,
            big,
            big,
            big,
            big,
            big,
            big,
            big,
            pltpu.VMEM((2 * T, TA), BF),
            big,
            big,
            big,
            big,
            pltpu.VMEM((D // 128, NB * GAP, 128), F32),
            pltpu.VMEM((D // 128, NB * GAP, 128), F32),
            pltpu.VMEM((2, 2 * NB, 2 * NB), BF),
            pltpu.VMEM((2, 2 * NB, 2 * NB), BF),
            pltpu.VMEM((2 * SINK, 2, 2 * NB, 2 * NB), F32),
            pltpu.VMEM((NB, D), F32),
            pltpu.VMEM((2, 2 * NB, 2 * NB), F32),
            pltpu.VMEM((2, NB, 128), BF),
            big,
            big,
            pltpu.VMEM((6 * 4096, 128), BF),
            pltpu.VMEM((max(1024, 32 * dp), 128), BF),
            pltpu.VMEM((16, D), F32),
            pltpu.VMEM((copies, 16, D), F32),
            pltpu.SemaphoreType.DMA((5,)),
            pltpu.SemaphoreType.DMA((12,)),
            pltpu.SemaphoreType.DMA((12, 8)),
            pltpu.SemaphoreType.DMA((10,)),
            pltpu.SemaphoreType.DMA((2,)),
            pltpu.SemaphoreType.DMA((1,)),
        ],
        compiler_params=pltpu.CompilerParams(
            vmem_limit_bytes=64 * 1024 * 1024, collective_id=0, has_side_effects=True
        ),
    )(lengths, tokens, cotangent, w_qkv, w_out, w_sort, *vectors, w_up, b_up, w_down)


def widen_kernel(
    ends_i, grads_i, sort_i, vec_i, ends_o, gup_o, gdown_o, gqkv_o, gout_o, gsort_o, v0_o, v1_o, v2_o, v3_o, v4_o, bup_o,
    ein, gin, zin, est, gst, esem, gsem, zsem, eout, gout,
):
    rows_e = 256
    steps = 2 * T // rows_e

    def e_in(i):
        rows = pl.ds(pl.multiple_of(i * rows_e, rows_e), rows_e)
        return pltpu.make_async_copy(ends_i.at[rows], ein.at[rows], esem.at[i])

    def g_in(p):
        rows = pl.ds(pl.multiple_of(p * 4096, 4096), 4096)
        return pltpu.make_async_copy(grads_i.at[rows], gin.at[rows], gsem.at[p])

    def e_out(i, count=rows_e, skip=0):
        rows = pl.ds(pl.multiple_of(i * rows_e + skip, count), count)
        slot = lax.rem(i, 8)
        part = est.at[slot, pl.ds(skip, count)]
        return pltpu.make_async_copy(part, ends_o.at[0, rows], eout.at[slot])

    jobs = []
    for p in range(4):
        part = pl.ds(p * FC, FC)
        jobs.append((p, gin, p * 4096, 4, gup_o.at[:, part]))
        jobs.append((p, gin, p * 4096 + 2048, 4, gdown_o.at[part]))
    jobs.append((4, gin, GOUT, 4, gout_o))
    for g, base in enumerate((GQ0, GQ1)):
        for at, n in enumerate(ORDER[g]):
            jobs.append((5, gin, base + at * 1024, 2, gqkv_o.at[:, pl.ds(n * D + g * GL, GL)]))
    jobs.append((6, zin, 0, 2, gsort_o))

    def job_out(n, count=D, skip=0):
        _, _, _, tiles, to = jobs[n]
        rows = pl.ds(skip, count)
        part = gst.at[n % 5, rows, pl.ds(0, tiles * 128)]
        return pltpu.make_async_copy(part, to.at[rows], gout.at[n % 5])

    for i in range(steps):
        e_in(i).start()
    for p in range(6):
        g_in(p).start()
    z_in = pltpu.make_async_copy(sort_i.at[pl.ds(0, 1024)], zin, zsem.at[0])
    z_in.start()
    for n, vec_o in zip((8, 9, 0, 1, 2), (v0_o, v1_o, v2_o, v3_o, v4_o)):
        vec_o[...] = vec_i[n : n + 1]
    for n in range(4):
        bup_o[:, n * D : (n + 1) * D] = vec_i[4 + n : 5 + n]

    @pl.loop(0, steps)
    def _(i):
        @pl.when(i >= 8)
        def _():
            e_out(i - 8).wait()

        e_in(i).wait()
        rows = pl.ds(pl.multiple_of(i * rows_e, rows_e), rows_e)
        est[lax.rem(i, 8)] = ein[rows].astype(F32)
        for n in range(2):
            e_out(i, rows_e // 2, n * (rows_e // 2)).start()

    z_in.wait()
    for n, (p, source, base, tiles, _) in enumerate(jobs):
        if p < 5 and (n == 0 or jobs[n - 1][0] != p):
            g_in(p).wait()
        if n == 8:
            g_in(5).wait()
        if n >= 5:
            job_out(n - 5).wait()
        for c in range(tiles):
            gst[n % 5, :, c * 128 : (c + 1) * 128] = source[
                base + c * 512 : base + (c + 1) * 512
            ].astype(F32)
        for m in range(4):
            job_out(n, D // 4, m * (D // 4)).start()
    for n in range(len(jobs) - 5, len(jobs)):
        job_out(n).wait()
    for i in range(steps - 8, steps):
        e_out(i).wait()


def widen(ends, grads, sort, vec):
    sds = jax.ShapeDtypeStruct
    return pl.pallas_call(
        widen_kernel,
        out_shape=(
            sds((1, 2 * T, D), F32),
            sds((D, FF), F32),
            sds((FF, D), F32),
            sds((D, 3 * D), F32),
            sds((D, D), F32),
            sds((D, HEADS * SPAN), F32),
        )
        + (sds((1, D), F32),) * 5
        + (sds((1, FF), F32),),
        in_specs=[HB] * 3 + [VM],
        out_specs=(HB,) * 6 + (VM,) * 6,
        scratch_shapes=[
            pltpu.VMEM((2 * T, D), BF),
            pltpu.VMEM((6 * 4096, 128), BF),
            pltpu.VMEM((1024, 128), BF),
            pltpu.VMEM((8, 256, D), F32),
            pltpu.VMEM((5, D, D), F32),
            pltpu.SemaphoreType.DMA((16,)),
            pltpu.SemaphoreType.DMA((6,)),
            pltpu.SemaphoreType.DMA((1,)),
            pltpu.SemaphoreType.DMA((8,)),
            pltpu.SemaphoreType.DMA((5,)),
        ],
        compiler_params=pltpu.CompilerParams(vmem_limit_bytes=62 * 1024 * 1024),
    )(ends, grads, sort, vec)


def shards(
    dp,
    tokens,
    lengths,
    w_qkv,
    w_out,
    w_sort,
    gain_attn,
    bias_attn,
    gain_ffn,
    bias_ffn,
    w_up,
    bias_up,
    w_down,
    bias_down,
    cotangent,
):
    vectors = [v[None] for v in (gain_attn, bias_attn, gain_ffn, bias_ffn, bias_down)]
    results = layer(
        dp,
        tokens,
        cotangent,
        lengths,
        w_qkv,
        w_out,
        w_sort,
        vectors,
        w_up,
        bias_up[None],
        w_down,
    )
    ends, gup, gdown, gqkv, gout, gsort, *small = widen(*results)
    g_attn, b_attn, g_ffn, b_ffn, b_down, b_up = (v.reshape(-1) for v in small)
    return (
        ends,
        gqkv,
        gout,
        gsort,
        g_attn,
        b_attn,
        g_ffn,
        b_ffn,
        gup,
        b_up,
        gdown,
        b_down,
    )


def solution(mesh):
    rep = [P()] * 11
    return jax.shard_map(
        functools.partial(shards, mesh.shape["dp"]),
        mesh=mesh,
        in_specs=(P("dp", None), P("dp", None), *rep, P("dp", None)),
        out_specs=(P("section", "dp", None), *rep),
        check_vma=False,
    )
```

```python
import functools
import math

import jax
import jax.numpy as jnp
from jax import lax
from jax.experimental import pallas as pl
from jax.experimental.pallas import tpu as pltpu
from jax.sharding import PartitionSpec as P

D = 512
HEADS = 8
HDIM = 64
FF = 2048
BLK = 32
SINK = 8
SPAN = 32
T = 2048
NB = T // BLK
TA = 256
TF = 512
FC = 512
GL = 256
GOUT, GQ0, GQ1 = 16384, 18432, 21504
ORDER = ((0, 1, 2), (1, 0, 2))
PIECE = 512
GAP = BLK + 1
SCALE = 1.0 / math.sqrt(HDIM)
BF = jnp.bfloat16
F32 = jnp.float32


def dot(a, b):
    return jnp.dot(a, b, preferred_element_type=F32)


def dot_nt(a, b):
    return lax.dot_general(a, b, (((1,), (1,)), ((), ())), preferred_element_type=F32)


def iota(shape, axis):
    return lax.broadcasted_iota(jnp.int32, shape, axis)


def normalise(x):
    xc = x - jnp.mean(x, axis=-1, keepdims=True)
    rstd = lax.rsqrt(jnp.mean(xc * xc, axis=-1, keepdims=True) + 1e-5)
    return xc * rstd, rstd


def normalise_back(g, xhat, rstd, gain):
    gg = g * gain
    return rstd * (
        gg
        - jnp.mean(gg, axis=-1, keepdims=True)
        - xhat * jnp.mean(gg * xhat, axis=-1, keepdims=True)
    )


def spread_heads(x, low, high):
    a, b = x[:, :128], x[:, 128:]
    z = jnp.zeros_like(a)
    rows = ([a * low, z], [a * high, z], [z, b * low], [z, b * high])
    return jnp.concatenate([jnp.concatenate(r, axis=1) for r in rows], axis=0)


def take_heads(x, first):
    r = x.shape[0] // 4
    tiles = [
        jnp.where(first, x[2 * c * r : (2 * c + 1) * r, c * 128 : (c + 1) * 128],
                  x[(2 * c + 1) * r : (2 * c + 2) * r, c * 128 : (c + 1) * 128])
        for c in range(2)
    ]
    return jnp.concatenate(tiles, axis=1)


def spread_even(x, low, high):
    a, b = x[:, :128], x[:, 128:]
    rows = ([a * low, b * low], [a * high, b * high])
    return jnp.concatenate([jnp.concatenate(r, axis=1) for r in rows], axis=0)


def spread_pair(x):
    z = jnp.zeros_like(x[:, :128])
    rows = ([x[:, :128], z], [z, x[:, 128:]])
    return jnp.concatenate([jnp.concatenate(r, axis=1) for r in rows], axis=0)


def beside(ref, count, rows):
    return jnp.concatenate([ref[n * rows : (n + 1) * rows] for n in range(count)], axis=1)


def settle(x):
    y = x.reshape(2, NB, 2 * NB)
    y = y - jnp.max(y, axis=1, keepdims=True)
    ex = jnp.exp(y)
    tot = jnp.sum(ex, axis=1, keepdims=True)
    return (ex * inverse(tot)).reshape(x.shape), (y - jnp.log(tot)).reshape(x.shape)


def settle_back(g, p):
    tot = jnp.sum(g.reshape(2, NB, 2 * NB), axis=1, keepdims=True)
    return g - (p.reshape(2, NB, 2 * NB) * tot).reshape(g.shape)


def wide(acc, rows, lanes=range(D // 128)):
    return jnp.concatenate([acc[c, rows] for c in lanes], axis=1)


def put_wide(acc, rows, value):
    for c in range(value.shape[1] // 128):
        acc[c, rows] = value[:, c * 128 : (c + 1) * 128]


def add_wide(acc, rows, value):
    for c in range(value.shape[1] // 128):
        acc[c, rows] += value[:, c * 128 : (c + 1) * 128]


def block_rows(block):
    return pl.ds(block * GAP, BLK)


def get_blocks(acc, first, count, lanes=range(D // 128)):
    return jnp.concatenate([wide(acc, block_rows(first + n), lanes) for n in range(count)], axis=0)


def put_blocks(acc, first, value, lane=0):
    for n in range(value.shape[0] // BLK):
        for c in range(value.shape[1] // 128):
            part = value[n * BLK : (n + 1) * BLK, c * 128 : (c + 1) * 128]
            acc[lane + c, block_rows(first + n)] = part


def flat_rows(ref, base, step, count):
    parts = [ref[pl.ds(pl.multiple_of(base + c * step, 16), count)] for c in range(D // 128)]
    return jnp.concatenate(parts, axis=1)


def put_flat(ref, base, value):
    rows = value.shape[0]
    for c in range(value.shape[1] // 128):
        ref[pl.ds(pl.multiple_of(base + c * rows, 16), rows)] = value[:, c * 128 : (c + 1) * 128]


def inverse(x):
    r = pl.reciprocal(x, approx=True)
    return r * (2.0 - x * r)


def gelu_both(u):
    c = math.sqrt(2.0 / math.pi)
    e = -2.0 * c / math.log(2.0)
    u2 = u * u
    power = jnp.minimum(u * (e + (e * 0.044715) * u2), 120.0)
    half = pl.reciprocal(1.0 + jnp.exp2(power), approx=True)
    act = u * half
    slope = half + act * (1.0 - half) * (2.0 * c + (6.0 * c * 0.044715) * u2)
    return act, slope


AXES = {16: ((1, 2), (2, 2), (4, 4)), 128: ((1, 4), (32, 4), (4, 8))}


def axes_of(dp):
    if dp in AXES:
        return AXES[dp]
    a = max(n for n in range(1, dp + 1) if dp % (n * n) == 0)
    return (1, a), (a, a), (a * a, dp // (a * a))


class Links:
    def __init__(self, groups):
        self.sec, self.dp = lax.axis_index("section"), lax.axis_index("dp")
        self.levels = []
        for axes in groups:
            own = [lax.rem(lax.div(self.dp, stride), n) for stride, n in axes]
            me, scale = 0, 1
            for (_, n), at in zip(axes, own):
                me, scale = me + at * scale, scale * n
            self.levels.append((axes, own, me))
        self.sizes = [2] + [math.prod(n for _, n in axes) for axes in groups]
        self.first = [0]
        for n in self.sizes:
            self.first.append(self.first[-1] + n - 1)
        self.copies = self.first[-1]

    def place(self, level, k):
        return lax.rem(self.levels[level - 1][2] + k, self.sizes[level])

    def peer(self, level, k):
        if level == 0:
            return (1 - self.sec, self.dp)
        axes, own, _ = self.levels[level - 1]
        place, to = self.place(level, k), self.dp
        for (stride, n), at in zip(axes, own):
            to = to + (lax.rem(place, n) - at) * stride
            place = lax.div(place, n)
        return (self.sec, to)

    def everyone(self):
        return [
            self.peer(level, k)
            for level in range(len(self.sizes))
            for k in range(1, self.sizes[level])
        ]


def all_links(dp):
    a, b, c = axes_of(dp)
    sec = lax.axis_index("section")
    a1 = (a[0] + sec * (b[0] - a[0]), a[1])
    b1 = (b[0] + sec * (a[0] - b[0]), b[1])
    return Links([[a1], [b1], [c]]), Links([[a, b], [c]])


def copies_of(dp):
    a, b, c = axes_of(dp)
    return a[1] * b[1] + c[1] - 1


def remote(src, dst, ssem, rsem, device):
    return pltpu.make_async_remote_copy(
        src_ref=src,
        dst_ref=dst,
        send_sem=ssem,
        recv_sem=rsem,
        device_id=device,
        device_id_type=pl.DeviceIdType.MESH,
    )


class Packet:
    def __init__(self, links, ref, out, base, rows, inboxes, ssem, rsem, osem, number):
        self.links, self.ref, self.out, self.inboxes = links, ref, out, inboxes
        self.ssem, self.rsem, self.osem, self.number = ssem, rsem, osem, number
        self.deep = len(links.sizes)
        self.last = 2 * self.deep
        half = rows // 2
        self.size = [half]
        self.off = [base + links.sec * half]
        self.away = base + (1 - links.sec) * half
        self.inpos = [0, 0 if inboxes[0] is not inboxes[1] else half]
        for level in range(1, self.deep):
            n = links.sizes[level]
            self.size.append(self.size[-1] // n)
            self.off.append(self.off[-1] + links.place(level, 0) * self.size[-1])
            self.inpos.append(self.inpos[-1] + (n - 1) * self.size[-1])

    def rows(self, ref, off, level):
        return ref.at[pl.ds(pl.multiple_of(off, 16), self.size[level])]

    def landing(self, level, k, skip, count):
        box, base = self.inboxes[min(level, 1)]
        at = base + self.inpos[level] + (k - 1) * self.size[level] + skip
        return box, pl.ds(pl.multiple_of(at, 16), count)

    def pieces(self, level):
        count = -(-self.size[level] // PIECE)
        rows = self.size[level] // count
        return [(n * rows, rows) for n in range(count)]

    def reduce_start(self, level, k):
        off = self.away
        if level > 0:
            off = self.off[level - 1] + self.links.place(level, k) * self.size[level]
        for skip, count in self.pieces(level):
            box, rows = self.landing(level, k, skip, count)
            remote(
                self.ref.at[pl.ds(pl.multiple_of(off + skip, 16), count)],
                box.at[rows],
                self.ssem.at[self.number],
                self.rsem.at[self.number, level],
                self.links.peer(level, k),
            ).start()

    def gather_start(self, level, k):
        source = self.ref if level == self.deep - 1 else self.out
        for skip, count in self.pieces(level):
            rows = pl.ds(pl.multiple_of(self.off[level] + skip, 16), count)
            remote(
                source.at[rows],
                self.out.at[rows],
                self.ssem.at[self.number],
                self.rsem.at[self.number, self.deep + level],
                self.links.peer(level, k),
            ).start()

    def arrived(self, level, gathered):
        count = (self.links.sizes[level] - 1) * self.size[level]
        if count == 0:
            return
        if not gathered:
            box, rows = self.landing(level, 1, 0, count)
            what = box.at[rows]
        else:
            base = self.away if level == 0 else self.off[level - 1]
            what = self.out.at[pl.ds(pl.multiple_of(base, 16), count)]
        sem = self.rsem.at[self.number, level + (self.deep if gathered else 0)]
        remote(what, what, self.ssem.at[self.number], sem, self.links.peer(0, 1)).wait_recv()

    def sent(self, source):
        count = 2 * sum((n - 1) * size for n, size in zip(self.links.sizes, self.size))
        what = source.at[pl.ds(0, count)]
        sem = self.rsem.at[self.number, 0]
        remote(what, what, self.ssem.at[self.number], sem, self.links.peer(0, 1)).wait_send()

    def own_copy(self):
        return pltpu.make_async_copy(
            self.rows(self.ref, self.off[-1], -1),
            self.rows(self.out, self.off[-1], -1),
            self.osem.at[self.number],
        )

    def ks(self, level):
        return range(1, self.links.sizes[level])

    def add(self, level):
        size = self.size[level]
        chunk = size // -(-size // 1024)
        wide_sum = self.links.sizes[level] > 2

        @pl.loop(0, size // chunk)
        def _(j):
            rows = pl.ds(pl.multiple_of(self.off[level] + j * chunk, 16), chunk)
            total = self.ref[rows]
            if wide_sum:
                total = total.astype(F32)
            for k in self.ks(level):
                box, came = self.landing(level, k, j * chunk, chunk)
                total += box[came].astype(total.dtype)
            self.ref[rows] = total.astype(BF)

    def step(self, n):
        deep = self.deep
        if 1 <= n <= deep:
            self.arrived(n - 1, False)
            self.add(n - 1)
        if n == deep:
            self.own_copy().start()
        if n == deep + 1:
            self.own_copy().wait()
        if n > deep:
            self.arrived(self.last - n, True)
        if n < deep:
            for k in self.ks(n):
                self.reduce_start(n, k)
        elif n < self.last:
            for k in self.ks(self.last - 1 - n):
                self.gather_start(self.last - 1 - n, k)


PLAN = {
    ("ffnend", 0): (("f0", 0),),
    ("ffn", 1, 2): (("f0", 1),),
    ("ffnend", 1): (("f1", 0),),
    ("ffn", 2, 2): (("f1", 1), ("f0", 2),),
    ("ffnend", 2): (("f2", 0),),
    ("ffn", 3, 1): (("f1", 2),),
    ("ffn", 3, 2): (("f2", 1), ("f0", 3),),
    ("ffnend", 3): (("f1", 3), ("f3", 0),),
    ("six", 3): (("f2", 2),),
    ("six", 4): (("f3", 1),),
    ("six", 6): (("f0", 4),),
    ("sixend",): (("o", 0),),
    ("seven", 0, 3): (("f1", 4),),
    ("seven", 0, 4): (("f2", 3), ("o", 1),),
    ("seven", 0, 5): (("f3", 2),),
    ("eight", 0, 0): (("f0", 5),),
    ("eight", 0, 3): (("o", 2),),
    ("nine", 0): (("f3", 3), ("f1", 5), ("q0", 0),),
    ("seven", 1, 0): (("f0", 6),),
    ("seven", 1, 2): (("f2", 4),),
    ("seven", 1, 3): (("o", 3), ("q0", 1),),
    ("seven", 1, 4): (("f1", 6),),
    ("eight", 1, 0): (("f3", 4),),
    ("eight", 1, 1): (("f0", 7),),
    ("nine", 1): (("qv", 0),),
    ("eight", 2, 0): (("q0", 2),),
    ("eight", 2, 1): (("f2", 5),),
    ("eight", 2, 2): (("f0", 8),),
    ("eight", 2, 3): (("o", 4),),
    ("nine", 2): (("qv", 1), ("f1", 7), ("qk", 0),),
    ("ten",): (("q0", 3), ("f3", 5), ("f2", 6), ("z2", 0),),
    ("eleven", 0): (("f1", 8), ("qk", 1), ("o", 5),),
    ("eleven", 1): (("qv", 2), ("z2", 1),),
    ("eleven", 2): (("f3", 6),),
    ("eleven", 3): (("q0", 4),),
    ("eleven", 5): (("f2", 7),),
    ("eleven", 7): (("qv", 3),),
    ("tail",): (
        ("va", 0), ("o", 6), ("qk", 2), ("f2", 8), ("va", 1), ("z2", 2), ("q0", 5), ("f3", 7),
        ("qv", 4), ("qk", 3), ("o", 7), ("va", 2), ("z2", 3), ("q0", 6), ("f3", 8), ("o", 8),
        ("qk", 4), ("va", 3), ("qv", 5), ("z2", 4), ("q0", 7), ("qv", 6), ("qk", 5), ("q0", 8),
        ("z2", 5), ("qk", 6), ("z2", 6),
    ),
}


def kernel(
    dp,
    len_ref,
    tok_ref,
    cot_ref,
    wqkv_ref,
    wout,
    wsort,
    gain_a_ref,
    bias_a_ref,
    gain_f_ref,
    bias_f_ref,
    bias_d_ref,
    wup,
    bup,
    wdown,
    ends_o,
    grads_o,
    sort_o,
    vec_o,
    xs,
    wqkv,
    w1,
    w2,
    cs,
    qs,
    ks,
    vs,
    kts,
    vts,
    kfs,
    vfs,
    ps,
    attt,
    mid,
    nf,
    nft,
    cott,
    acc0,
    acc1,
    mcat,
    mcatt,
    psave,
    summ,
    gm,
    halves,
    actb,
    gpreb,
    gr,
    gz,
    vb,
    vin,
    sem_in,
    ssem,
    rsem,
    out_sem,
    end_send,
    end_recv,
):
    deep, flat = all_links(dp)
    sec = deep.sec
    mine = pl.ds(pl.multiple_of(sec * T, T), T)
    for c in range(4):
        lanes = slice(c * 128, (c + 1) * 128)
        pltpu.make_async_copy(
            tok_ref.at[mine, lanes], xs.at[pl.ds(c * T, T)], sem_in.at[0]
        ).start()
    e0 = len_ref[sec, 0]
    e1 = e0 + len_ref[sec, 1]
    gain_a, bias_a = gain_a_ref[...], bias_a_ref[...]
    gain_f, bias_f = gain_f_ref[...], bias_f_ref[...]
    bias_d = bias_d_ref[...]
    vb[...] = jnp.zeros_like(vb)
    w_copy = pltpu.make_async_copy(wqkv_ref, wqkv, sem_in.at[4])
    w_copy.start()
    x_part = xs.at[pl.ds(0, 4 * T)]
    pltpu.make_async_copy(x_part, x_part, sem_in.at[0]).wait()
    w_copy.wait()
    cot_copy = pltpu.make_async_copy(cot_ref.at[mine], cs, sem_in.at[1])
    cot_copy.start()
    for c in range(FF // FC):
        for l in range(4):
            to = pl.ds((c * 4 + l) * FC, FC)
            lane = l * 128
            pltpu.make_async_copy(
                wup.at[:, pl.ds(c * FC + lane, 128)], w1.at[to], sem_in.at[2]
            ).start()
            pltpu.make_async_copy(
                wdown.at[pl.ds(c * FC, FC), pl.ds(lane, 128)], w2.at[to], sem_in.at[3]
            ).start()

    def packet(number, base, rows, links, box, more=None, ref=gr, out=grads_o):
        boxes = (box, box if more is None else more)
        return Packet(links, ref, out, base, rows, boxes, ssem, rsem, out_sem, number)

    boxes = ((xs, 0), (xs, 4096), (w1, 0), (w2, 0))
    f = [packet(p, p * 4096, 4096, deep, boxes[p]) for p in range(4)]
    parts = dict(f0=f[0], f1=f[1], f2=f[2], f3=f[3])
    if 1024 % (32 * dp) == 0:
        parts["o"] = packet(4, GOUT, 2048, deep, (w1, 4096))
        parts["q0"] = packet(5, GQ0, 3072, deep, (w2, 4096))
        parts["qk"] = packet(6, GQ1, 1024, flat, (w1, 0))
        parts["qv"] = packet(7, GQ1 + 1024, 2048, flat, (w1, 6144))
        parts["z2"] = packet(9, 0, 1024, flat, (w2, 7168), ref=gz, out=sort_o)
    else:
        parts["qk"] = packet(4, GOUT, 8192, flat, (w1, 0))
        parts["z2"] = packet(5, 0, gz.shape[0], flat, (w2, 4096), ref=gz, out=sort_o)

    class Vectors:
        def __init__(self, number, base, count):
            self.number, self.rows = number, pl.ds(base, count)

        def copy(self, level, k):
            at = flat.first[level] + k - 1
            return remote(
                vb.at[self.rows],
                vin.at[at, self.rows],
                ssem.at[self.number],
                rsem.at[self.number, level],
                flat.peer(level, k),
            )

        def step(self, n):
            if n >= 1:
                first, count = flat.first[n - 1], flat.sizes[n - 1] - 1
                if count:
                    came = vin.at[pl.ds(first, count), self.rows]
                    sem = rsem.at[self.number, n - 1]
                    both = remote(came, came, ssem.at[self.number], sem, flat.peer(0, 1))
                    both.wait_send()
                    both.wait_recv()
                for k in range(count):
                    vb[self.rows] += vin[first + k, self.rows]
            if n < len(flat.sizes):
                for k in range(1, flat.sizes[n]):
                    self.copy(n, k).start()

    packets = list(parts.values())
    parts["va"] = Vectors(10, 0, 16)
    def steps(*where):
        for name, n in PLAN.get(where, ()):
            if name in parts:
                parts[name].step(n)

    def steps_at(i, *where):
        for place in PLAN:
            if place[:-1] == where:

                @pl.when(i == place[-1])
                def _():
                    steps(*place)

    def end_copies(at, count, far_sec, staged):
        tile = staged.at[pl.ds(pl.multiple_of(at, TA), count)]
        there = ends_o.at[pl.ds(pl.multiple_of(sec * T + at, TA), count)]
        away = remote(tile, there, end_send.at[far_sec], end_recv.at[0], flat.peer(0, 1))
        return away, pltpu.make_async_copy(tile, there, end_send.at[far_sec])

    def put_end(i, far_sec, staged):
        away, here = end_copies(i * TA, TA, far_sec, staged)

        @pl.when(sec == far_sec)
        def _():
            away.start()

        @pl.when(sec != far_sec)
        def _():
            here.start()

    def wait_end(far_sec, staged):
        away, here = end_copies(0, T, far_sec, staged)

        @pl.when(sec == far_sec)
        def _():
            away.wait_send()

        @pl.when(sec != far_sec)
        def _():
            here.wait()

    lane = iota((NB, 128), 1)
    halves[0] = (lane < HDIM).astype(BF)
    halves[1] = (lane >= HDIM).astype(BF)

    @pl.loop(0, T // TA)
    def _(i):
        rows = pl.ds(pl.multiple_of(i * TA, TA), TA)
        xhat, _ = normalise(flat_rows(xs, i * TA, T, TA).astype(F32))
        normed = xhat * gain_a + bias_a
        low = normed.astype(BF)
        packed = dot(low, wqkv[...]).astype(BF)
        qs[rows] = packed[:, :D]
        k, v = packed[:, D : 2 * D], packed[:, 2 * D :]
        ks[rows] = k
        vs[rows] = v
        nb = TA // BLK
        put_blocks(acc0, i * nb, k.astype(F32))
        put_blocks(acc1, i * nb, v.astype(F32))
        summ[pl.ds(pl.multiple_of(i * nb, nb), nb)] = jnp.mean(
            normed.reshape(nb, BLK, D), axis=1
        )

    blk = iota((2 * NB, 2 * NB), 0) & (NB - 1)
    col = iota((2 * NB, 2 * NB), 1) & (NB - 1)
    owner = (blk >= e0).astype(jnp.int32) + (blk >= e1).astype(jnp.int32)
    col_owner = (col >= e0).astype(jnp.int32) + (col >= e1).astype(jnp.int32)
    same = owner == col_owner
    allowed = same & (col <= blk)
    before = same & (col < blk)
    a = iota((HEADS * SPAN, D), 0)
    b = iota((HEADS * SPAN, D), 1)
    gap = jnp.where(a >> 5 == b >> 6, (b & (HDIM - 1)) - (a & (SPAN - 1)), -1000)
    row = iota((NB, D), 0)
    firsts = (jnp.int32(0), e0, e1)
    lasts = (e0, e1, jnp.int32(NB))
    logits = dot(summ[...].astype(BF), wsort[...])
    high = logits.astype(BF)
    rest = logits - high.astype(F32)
    middle = rest.astype(BF)
    three = jnp.concatenate([high, middle, (rest - middle.astype(F32)).astype(BF)], axis=0)
    placed = jnp.zeros((NB, D), F32)
    for s in range(3):
        moved = dot(three, (gap == firsts[s]).astype(BF))
        moved = moved[:NB] + moved[NB : 2 * NB] + moved[2 * NB :]
        placed = jnp.where(row >= firsts[s], moved, placed)
    start = []
    for g in range(2):
        tiles = [placed[:, c : c + 128] for c in (2 * g * 128, (2 * g + 1) * 128)]
        start.append(jnp.where(allowed, jnp.concatenate(tiles, axis=0), -10000.0))

    def sweep(it, cur):
        for n in range(2):
            cur = [x.T for x in cur]
            done = [settle(x) for x in cur]
            for g in range(2):
                psave[2 * it + n, g] = done[g][0]
            cur = [x for _, x in done]
        return tuple(cur)

    lax.fori_loop(0, SINK, sweep, tuple(start))
    for g in range(2):
        mix = jnp.where(before, psave[2 * SINK - 1, g], 0.0)
        mcat[g] = mix.astype(BF)
        for p in range(2):
            tr = mix[p * NB : (p + 1) * NB].T.astype(BF)
            mcatt[g, p * NB : (p + 1) * NB] = jnp.concatenate([tr[:NB], tr[NB:]], axis=1)

    @pl.loop(0, BLK // 4)
    def _(it):
        low, high = halves[0], halves[1]
        jobs, outs = [], []
        for u in range(4):
            t = it * 4 + u
            every = pl.ds(t, NB, stride=GAP)
            for acc, keep in ((acc0, kts), (acc1, vts)):
                x = wide(acc, every).astype(BF)
                keep[pl.ds(pl.multiple_of(t * NB, NB), NB)] = x
                jobs.append((acc, every, x))
        for acc, every, x in jobs:
            for g in range(2):
                far = dot(mcat[g], spread_even(x[:, g * GL : (g + 1) * GL], low, high))
                outs.append((acc, every, g, far))
        for acc, every, g, far in outs:
            acc[2 * g, every] = far[:NB, :128].astype(BF).astype(F32)
            acc[2 * g + 1, every] = far[NB:, 128:].astype(BF).astype(F32)

    pair = 2 * BLK
    srow = iota((2 * pair, GL), 0)
    tcol = iota((2 * pair, GL), 1) & (pair - 1)
    together = (srow & BLK) == (tcol & BLK)
    own_ok = together & (srow < pair) & ((srow & (BLK - 1)) <= (tcol & (BLK - 1)))
    far_ok = together & (srow >= pair)

    cot_copy.wait()

    @pl.loop(0, T // TA)
    def _(i):
        low, high = halves[0], halves[1]
        first = iota((pair, 128), 1) < HDIM
        seen, scores = [], []
        for j in range(TA // pair):
            block = (i * (TA // pair) + j) * 2
            rows = pl.ds(pl.multiple_of(block * BLK, pair), pair)
            kf = get_blocks(acc0, block, 2).astype(BF)
            vf16 = get_blocks(acc1, block, 2).astype(BF)
            kfs[rows] = kf
            vfs[rows] = vf16
            kseen = jnp.concatenate([ks[rows], kf], axis=0)
            seen.append(jnp.concatenate([vs[rows], vf16], axis=0))
            q = qs[rows] * SCALE
            closed = []
            for n in (block, block + 1):
                opening = (n == 0) | (n == e0) | (n == e1)
                closed.append(jnp.where(opening, 0, 1))
            open_far = jnp.where(tcol < BLK, closed[0], closed[1]) == 1
            valid = own_ok | (far_ok & open_far)
            for g in range(2):
                lanes = slice(g * GL, (g + 1) * GL)
                sc = dot_nt(kseen[:, lanes], spread_heads(q[:, lanes], low, high))
                scores.append(jnp.where(valid, sc, -1e9))
        sc = jnp.concatenate(scores, axis=1)
        ex = jnp.exp(sc - jnp.max(sc, axis=0, keepdims=True))
        w16 = (ex * inverse(jnp.sum(ex, axis=0, keepdims=True))).astype(BF)
        ws = [w16[:, c : c + GL] for c in range(0, w16.shape[1], GL)]
        turned = [w.T for w in ws]
        for n, w in enumerate(ws):
            prow = pl.ds(pl.multiple_of((i * (TA // pair) + n // 2) * pair, pair), pair)
            kept = [w[c : c + BLK] + w[c + BLK : c + pair] for c in (0, pair)]
            ps[prow, n % 2 * GL : (n % 2 + 1) * GL] = jnp.concatenate(kept, axis=0)
        products = [
            dot(w, seen[n // 2][:, n % 2 * GL : (n % 2 + 1) * GL]) for n, w in enumerate(turned)
        ]
        made = [take_heads(r, first).astype(BF) for r in products]
        rows = pl.ds(pl.multiple_of(i * TA, TA), TA)
        att = jnp.concatenate(
            [jnp.concatenate(made[n : n + 2], axis=1) for n in range(0, len(made), 2)], axis=0
        )
        for n in range(2):
            at = pl.multiple_of(i * D + n * TA, TA)
            attt[pl.ds(at, TA)] = att[:, n * TA : (n + 1) * TA]
        x = flat_rows(xs, i * TA, T, TA).astype(F32)
        middle = (x + dot(att, wout[...])).astype(BF)
        mid[rows] = middle
        xhat, _ = normalise(middle.astype(F32))
        nf[rows] = (xhat * gain_f + bias_f).astype(BF)

    barrier = pltpu.get_barrier_semaphore()
    everyone = flat.everyone()
    for device in everyone:
        pl.semaphore_signal(
            barrier, inc=1, device_id=device, device_id_type=pl.DeviceIdType.MESH
        )

    @pl.loop(0, T // TF)
    def _(i):
        rows = pl.ds(pl.multiple_of(i * TF, TF), TF)
        nft[rows] = nf[rows].T
        cott[rows] = cs[rows].T
        put_wide(acc0, rows, jnp.zeros((TF, D), F32))
        put_wide(acc1, rows, jnp.zeros((TF, D), F32))

    pltpu.make_async_copy(w1, w1, sem_in.at[2]).wait()
    pltpu.make_async_copy(w2, w2, sem_in.at[3]).wait()
    pl.semaphore_wait(barrier, len(everyone))

    @pl.loop(0, FF // FC)
    def _(c):
        cols = pl.ds(pl.multiple_of(c * FC, FC), FC)
        @pl.loop(0, T // TF)
        def _(i):
            rows = pl.ds(pl.multiple_of(i * TF, TF), TF)
            up = flat_rows(w1, c * 4 * FC, FC, FC)
            down = flat_rows(w2, c * 4 * FC, FC, FC)
            pre = dot(nf[rows], up) + bup[0:1, cols]
            act, slope = gelu_both(pre)
            act = act.astype(BF)
            gact = dot_nt(cs[rows], down)
            gpre = slope * gact
            vb[pl.ds(4 + c, 1)] += jnp.sum(gpre, axis=0, keepdims=True)
            gpre = gpre.astype(BF)
            add_wide(acc0, rows, dot(act, down))
            add_wide(acc1, rows, dot_nt(gpre, up))
            actb[rows] = act
            gpreb[rows] = gpre
            for chunk in range(FF // FC):

                @pl.when(c == chunk)
                def _():
                    steps_at(i, "ffn", chunk)

        gu = dot(beside(nft, T // TF, D), gpreb[...])
        put_flat(gr, c * 4096, gu.astype(BF))
        gd = dot(beside(cott, T // TF, D), actb[...])
        put_flat(gr, c * 4096 + 2048, gd.T.astype(BF))

        steps_at(c, "ffnend")


    @pl.loop(0, T // TA)
    def _(i):
        rows = pl.ds(pl.multiple_of(i * TA, TA), TA)
        mf = mid[rows].astype(F32)
        gpreb[rows] = (mf + wide(acc0, rows) + bias_d).astype(BF)
        put_end(i, 0, gpreb)
        cot = cs[rows].astype(F32)
        gn = wide(acc1, rows)
        xhat, rstd = normalise(mf)
        vb[0:1] += jnp.sum(gn * xhat, axis=0, keepdims=True)
        vb[1:2] += jnp.sum(gn, axis=0, keepdims=True)
        vb[2:3] += jnp.sum(cot, axis=0, keepdims=True)
        nf[rows] = (cot + normalise_back(gn, xhat, rstd, gain_f)).astype(BF)
        steps_at(i, "six")

    x_copy = pltpu.make_async_copy(tok_ref.at[mine], cs, sem_in.at[0])
    x_copy.start()
    for n in range(T // TA):
        tile = [attt[n * D + m * TA : n * D + (m + 1) * TA] for m in range(2)]
        attt[n * D : (n + 1) * D] = jnp.concatenate(tile, axis=1).T
    gout = dot(beside(attt, T // TA, D), nf[...]).astype(BF)
    put_flat(gr, GOUT, gout)
    gm[...] = jnp.zeros_like(gm)
    steps("sixend")
    x_copy.wait()

    for g in range(2):
        lanes = slice(g * GL, (g + 1) * GL)
        base = (GQ0, GQ1)[g]

        @pl.loop(0, T // TA)
        def _(i):
            rows_t = pl.ds(pl.multiple_of(i * TA, TA), TA)
            gat = dot_nt(nf[rows_t], wout[lanes]).astype(BF)
            low, high = halves[0], halves[1]
            first = iota((pair, 128), 1) < HDIM
            block0 = (iota((BLK, GL), 1) & BLK == 0).astype(BF)
            block1 = (iota((BLK, GL), 1) & BLK != 0).astype(BF)
            blocks, spread, gws, w16s = [], [], [], []
            for j in range(TA // pair):
                at = pl.multiple_of((i * (TA // pair) + j) * pair, pair)
                rows = pl.ds(at, pair)
                vseen = jnp.concatenate([vs[rows, lanes], vfs[rows, lanes]], axis=0)
                gad = spread_heads(gat[j * pair : (j + 1) * pair], low, high)
                gws.append(dot_nt(vseen, gad))
                kept = ps[rows, lanes]
                own, far = kept[:BLK], kept[BLK:]
                w16s.append(
                    jnp.concatenate(
                        [own * block0, own * block1, far * block0, far * block1], axis=0
                    )
                )
                blocks.append(rows)
                spread.append(gad)
            w16 = jnp.concatenate(w16s, axis=1)
            gw = jnp.concatenate(gws, axis=1)
            w = w16.astype(F32)
            gs = w * (gw - jnp.sum(gw * w, axis=0, keepdims=True))
            gs = (gs * SCALE).astype(BF)
            gss = [gs[:, c : c + GL] for c in range(0, gs.shape[1], GL)]
            turned = [part.T for part in gss]
            gvs = [dot(w, gad).astype(BF) for w, gad in zip(w16s, spread)]
            gks = [
                dot(part, spread_heads(qs[rows, lanes], low, high)).astype(BF)
                for part, rows in zip(gss, blocks)
            ]
            gqs = []
            for part, rows in zip(turned, blocks):
                kseen = jnp.concatenate([ks[rows, lanes], kfs[rows, lanes]], axis=0)
                gqs.append(dot(part, kseen))
            for j, (rows, gk, gv, gq) in enumerate(zip(blocks, gks, gvs, gqs)):
                block = (i * (TA // pair) + j) * 2
                cott[rows, lanes] = gk[:pair]
                mid[rows, lanes] = gv[:pair]
                put_blocks(acc0, block, gk[pair:].astype(F32), 2 * g)
                put_blocks(acc1, block, gv[pair:].astype(F32), 2 * g)
                nft[rows, lanes] = take_heads(gq, first).astype(BF)
            if g == 0:
                xhat, _ = normalise(cs[rows_t].astype(F32))
                nl = (xhat * gain_a + bias_a).astype(BF)
                attt[pl.ds(pl.multiple_of(i * D, D), D)] = nl.T
            steps_at(i, "seven", g)

        gq = dot(beside(attt, T // TA, D), nft[:, lanes]).astype(BF)
        put_flat(gr, base + ORDER[g].index(0) * 1024, gq)
        steps("sevenend", g)

        keys, values = (acc0, kts, cott, 1), (acc1, vts, mid, 2)
        for turn, both in enumerate(((keys, values),) if g == 0 else ((values,), (keys,))):
            count = 8 // len(both)

            @pl.loop(0, BLK // count)
            def _(it):
                low, high = halves[0], halves[1]
                jobs, outs = [], []
                for u in range(count):
                    t = it * count + u
                    every = pl.ds(t, NB, stride=GAP)
                    trow = pl.ds(pl.multiple_of(t * NB, NB), NB)
                    for acc, near, _, _ in both:
                        x = jnp.concatenate([acc[2 * g, every], acc[2 * g + 1, every]], axis=1)
                        jobs.append((acc, every, x.astype(BF), near[trow, lanes]))
                spread = [spread_even(x, low, high) for _, _, x, _ in jobs]
                nears = [spread_pair(n) for _, _, _, n in jobs]
                gm[g] += dot_nt(
                    jnp.concatenate(spread, axis=1), jnp.concatenate(nears, axis=1)
                )
                for (acc, every, _, _), x in zip(jobs, spread):
                    outs.append((acc, every, dot(mcatt[g], x)))
                for acc, every, back in outs:
                    acc[2 * g, every] = back[:NB, :128]
                    acc[2 * g + 1, every] = back[NB:, 128:]
                steps_at(it, "eight", g + turn)

            @pl.loop(0, T // TA)
            def _(i):
                rows = pl.ds(pl.multiple_of(i * TA, TA), TA)
                for acc, _, part, _ in both:
                    far = get_blocks(acc, i * (TA // BLK), TA // BLK, (2 * g, 2 * g + 1))
                    part[rows, lanes] = (part[rows, lanes].astype(F32) + far).astype(BF)

            nlt = beside(attt, T // TA, D)
            for _, _, part, n in both:
                at = base + ORDER[g].index(n) * 1024
                put_flat(gr, at, dot(nlt, part[:, lanes]).astype(BF))
            steps("nine", g + turn)

    grads = []
    for g in range(2):
        tiles = []
        for p in range(2):
            lanes = slice(p * NB, (p + 1) * NB)
            tiles.append(jnp.concatenate([gm[g, :NB, lanes], gm[g, NB:, lanes]], axis=1))
        grad = jnp.concatenate(tiles, axis=0) * psave[2 * SINK - 1, g]
        grads.append(jnp.where(before, grad, 0.0))

    def sweep_back(n, grads):
        it = SINK - 1 - n
        for m in (1, 0):
            grads = [settle_back(x, psave[2 * it + m, g]).T for g, x in enumerate(grads)]
        return tuple(grads)

    grads = lax.fori_loop(0, SINK, sweep_back, tuple(grads))
    grads = [jnp.where(allowed, x, 0.0) for x in grads]
    grad = jnp.concatenate([x[c : c + NB] for x in grads for c in (0, NB)], axis=1)
    glog = jnp.zeros((NB, HEADS * SPAN), F32)
    for s in range(3):
        mine_rows = (row >= firsts[s]) & (row < lasts[s])
        kept = jnp.where(mine_rows, grad, 0.0).astype(BF)
        glog = glog + dot_nt(kept, (gap == firsts[s]).astype(BF))
    glog = glog.astype(BF)
    if gz.shape[0] > 1024:
        gz[...] = jnp.zeros_like(gz)
    put_flat(gz, 0, dot(summ[...].astype(BF).T, glog).astype(BF))
    steps("ten")
    summ[...] = dot_nt(glog, wsort[...]) * (1.0 / BLK)

    @pl.loop(0, T // TA)
    def _(i):
        rows = pl.ds(pl.multiple_of(i * TA, TA), TA)
        gp = jnp.concatenate([nft[rows], cott[rows], mid[rows]], axis=1)
        nb = TA // BLK
        gs = summ[pl.ds(pl.multiple_of(i * nb, nb), nb)]
        gn = dot_nt(gp, wqkv[...]) + jnp.broadcast_to(
            gs[:, None, :], (nb, BLK, D)
        ).reshape(TA, D)
        xhat, rstd = normalise(cs[rows].astype(F32))
        vb[8:9] += jnp.sum(gn * xhat, axis=0, keepdims=True)
        vb[9:10] += jnp.sum(gn, axis=0, keepdims=True)
        gx = nf[rows].astype(F32) + normalise_back(gn, xhat, rstd, gain_a)
        actb[rows] = gx.astype(BF)
        put_end(i, 1, actb)
        steps_at(i, "eleven")

    steps("tail")
    vec_o[...] = vb[...]
    wait_end(0, gpreb)
    wait_end(1, actb)
    there = ends_o.at[pl.ds(pl.multiple_of((1 - sec) * T, T), T)]
    remote(there, there, end_send.at[0], end_recv.at[0], flat.peer(0, 1)).wait_recv()
    for part in packets:
        part.sent(gr)


VM = pl.BlockSpec(memory_space=pltpu.VMEM)
HB = pl.BlockSpec(memory_space=pl.ANY)
SM = pl.BlockSpec(memory_space=pltpu.SMEM)


def layer(dp, tokens, cotangent, lengths, w_qkv, w_out, w_sort, vectors, w_up, b_up, w_down):
    sds = jax.ShapeDtypeStruct
    big = pltpu.VMEM((T, D), BF)
    copies = copies_of(dp)
    return pl.pallas_call(
        functools.partial(kernel, dp),
        out_shape=(
            sds((2 * T, D), BF),
            sds((6 * 4096, 128), BF),
            sds((max(1024, 32 * dp), 128), BF),
            sds((16, D), F32),
        ),
        in_specs=[SM, HB, HB, HB] + [VM] * 7 + [HB, VM, HB],
        out_specs=(HB, HB, HB, VM),
        scratch_shapes=[
            pltpu.VMEM((8192, 128), BF),
            pltpu.VMEM((D, 3 * D), BF),
            pltpu.VMEM((8192, 128), BF),
            pltpu.VMEM((8192, 128), BF),
            big,
            big,
            big,
            big,
            big,
            big,
            big,
            big,
            big,
            pltpu.VMEM((2 * T, TA), BF),
            big,
            big,
            big,
            big,
            pltpu.VMEM((D // 128, NB * GAP, 128), F32),
            pltpu.VMEM((D // 128, NB * GAP, 128), F32),
            pltpu.VMEM((2, 2 * NB, 2 * NB), BF),
            pltpu.VMEM((2, 2 * NB, 2 * NB), BF),
            pltpu.VMEM((2 * SINK, 2, 2 * NB, 2 * NB), F32),
            pltpu.VMEM((NB, D), F32),
            pltpu.VMEM((2, 2 * NB, 2 * NB), F32),
            pltpu.VMEM((2, NB, 128), BF),
            big,
            big,
            pltpu.VMEM((6 * 4096, 128), BF),
            pltpu.VMEM((max(1024, 32 * dp), 128), BF),
            pltpu.VMEM((16, D), F32),
            pltpu.VMEM((copies, 16, D), F32),
            pltpu.SemaphoreType.DMA((5,)),
            pltpu.SemaphoreType.DMA((12,)),
            pltpu.SemaphoreType.DMA((12, 8)),
            pltpu.SemaphoreType.DMA((10,)),
            pltpu.SemaphoreType.DMA((2,)),
            pltpu.SemaphoreType.DMA((1,)),
        ],
        compiler_params=pltpu.CompilerParams(
            vmem_limit_bytes=64 * 1024 * 1024, collective_id=0, has_side_effects=True
        ),
    )(lengths, tokens, cotangent, w_qkv, w_out, w_sort, *vectors, w_up, b_up, w_down)


def widen_kernel(
    ends_i, grads_i, sort_i, vec_i, ends_o, gup_o, gdown_o, gqkv_o, gout_o, gsort_o, v0_o, v1_o, v2_o, v3_o, v4_o, bup_o,
    ein, gin, zin, est, gst, esem, gsem, zsem, eout, gout,
):
    rows_e = 256
    steps = 2 * T // rows_e

    def e_in(i):
        rows = pl.ds(pl.multiple_of(i * rows_e, rows_e), rows_e)
        return pltpu.make_async_copy(ends_i.at[rows], ein.at[rows], esem.at[i])

    def g_in(p):
        rows = pl.ds(pl.multiple_of(p * 4096, 4096), 4096)
        return pltpu.make_async_copy(grads_i.at[rows], gin.at[rows], gsem.at[p])

    def e_out(i, count=rows_e, skip=0):
        rows = pl.ds(pl.multiple_of(i * rows_e + skip, count), count)
        slot = lax.rem(i, 8)
        part = est.at[slot, pl.ds(skip, count)]
        return pltpu.make_async_copy(part, ends_o.at[0, rows], eout.at[slot])

    jobs = []
    for p in range(4):
        part = pl.ds(p * FC, FC)
        jobs.append((p, gin, p * 4096, 4, gup_o.at[:, part]))
        jobs.append((p, gin, p * 4096 + 2048, 4, gdown_o.at[part]))
    jobs.append((4, gin, GOUT, 4, gout_o))
    for g, base in enumerate((GQ0, GQ1)):
        for at, n in enumerate(ORDER[g]):
            jobs.append((5, gin, base + at * 1024, 2, gqkv_o.at[:, pl.ds(n * D + g * GL, GL)]))
    jobs.append((6, zin, 0, 2, gsort_o))

    def job_out(n, count=D, skip=0):
        _, _, _, tiles, to = jobs[n]
        rows = pl.ds(skip, count)
        part = gst.at[n % 5, rows, pl.ds(0, tiles * 128)]
        return pltpu.make_async_copy(part, to.at[rows], gout.at[n % 5])

    for i in range(steps):
        e_in(i).start()
    for p in range(6):
        g_in(p).start()
    z_in = pltpu.make_async_copy(sort_i.at[pl.ds(0, 1024)], zin, zsem.at[0])
    z_in.start()
    for n, vec_o in zip((8, 9, 0, 1, 2), (v0_o, v1_o, v2_o, v3_o, v4_o)):
        vec_o[...] = vec_i[n : n + 1]
    for n in range(4):
        bup_o[:, n * D : (n + 1) * D] = vec_i[4 + n : 5 + n]

    @pl.loop(0, steps)
    def _(i):
        @pl.when(i >= 8)
        def _():
            e_out(i - 8).wait()

        e_in(i).wait()
        rows = pl.ds(pl.multiple_of(i * rows_e, rows_e), rows_e)
        est[lax.rem(i, 8)] = ein[rows].astype(F32)
        for n in range(2):
            e_out(i, rows_e // 2, n * (rows_e // 2)).start()

    z_in.wait()
    for n, (p, source, base, tiles, _) in enumerate(jobs):
        if p < 5 and (n == 0 or jobs[n - 1][0] != p):
            g_in(p).wait()
        if n == 8:
            g_in(5).wait()
        if n >= 5:
            job_out(n - 5).wait()
        for c in range(tiles):
            gst[n % 5, :, c * 128 : (c + 1) * 128] = source[
                base + c * 512 : base + (c + 1) * 512
            ].astype(F32)
        for m in range(4):
            job_out(n, D // 4, m * (D // 4)).start()
    for n in range(len(jobs) - 5, len(jobs)):
        job_out(n).wait()
    for i in range(steps - 8, steps):
        e_out(i).wait()


def widen(ends, grads, sort, vec):
    sds = jax.ShapeDtypeStruct
    return pl.pallas_call(
        widen_kernel,
        out_shape=(
            sds((1, 2 * T, D), F32),
            sds((D, FF), F32),
            sds((FF, D), F32),
            sds((D, 3 * D), F32),
            sds((D, D), F32),
            sds((D, HEADS * SPAN), F32),
        )
        + (sds((1, D), F32),) * 5
        + (sds((1, FF), F32),),
        in_specs=[HB] * 3 + [VM],
        out_specs=(HB,) * 6 + (VM,) * 6,
        scratch_shapes=[
            pltpu.VMEM((2 * T, D), BF),
            pltpu.VMEM((6 * 4096, 128), BF),
            pltpu.VMEM((1024, 128), BF),
            pltpu.VMEM((8, 256, D), F32),
            pltpu.VMEM((5, D, D), F32),
            pltpu.SemaphoreType.DMA((16,)),
            pltpu.SemaphoreType.DMA((6,)),
            pltpu.SemaphoreType.DMA((1,)),
            pltpu.SemaphoreType.DMA((8,)),
            pltpu.SemaphoreType.DMA((5,)),
        ],
        compiler_params=pltpu.CompilerParams(vmem_limit_bytes=62 * 1024 * 1024),
    )(ends, grads, sort, vec)


def shards(
    dp,
    tokens,
    lengths,
    w_qkv,
    w_out,
    w_sort,
    gain_attn,
    bias_attn,
    gain_ffn,
    bias_ffn,
    w_up,
    bias_up,
    w_down,
    bias_down,
    cotangent,
):
    vectors = [v[None] for v in (gain_attn, bias_attn, gain_ffn, bias_ffn, bias_down)]
    results = layer(
        dp,
        tokens,
        cotangent,
        lengths,
        w_qkv,
        w_out,
        w_sort,
        vectors,
        w_up,
        bias_up[None],
        w_down,
    )
    ends, gup, gdown, gqkv, gout, gsort, *small = widen(*results)
    g_attn, b_attn, g_ffn, b_ffn, b_down, b_up = (v.reshape(-1) for v in small)
    return (
        ends,
        gqkv,
        gout,
        gsort,
        g_attn,
        b_attn,
        g_ffn,
        b_ffn,
        gup,
        b_up,
        gdown,
        b_down,
    )


def solution(mesh):
    rep = [P()] * 11
    return jax.shard_map(
        functools.partial(shards, mesh.shape["dp"]),
        mesh=mesh,
        in_specs=(P("dp", None), P("dp", None), *rep, P("dp", None)),
        out_specs=(P("section", "dp", None), *rep),
        check_vma=False,
    )
```
